32 devices in a mesh: samp: 4 (over z), arow: 4 (over y, x), acol: 2 (over core).
Axes of the slice: x: 2, y: 2, z: 4, core: 2. Of those that a mesh axis runs over, the one named last changes fastest.
Arguments:
- embeddings: bfloat16 [49152, 768], P(('samp', 'arow', 'acol')), may hold values from -6 to 6
- anchors: bfloat16 [16384, 768], P(('arow', 'acol')), may hold values from -6 to 6
- subspace: bfloat16 [16384, 64], P(('arow', 'acol')), may hold values from -3 to 3
- nearest: int32 [49152, 8], P(('samp', 'arow', 'acol')), may hold values from 0 to 16383, as said below
Outputs:
- gram_product: float32 [16384, 64], P(('arow', 'acol'))
The draws below stay inside these ranges and needn't reach their ends.
Inputs may be any that keep to these rules, and one draw needn't show every extreme that they name: `nearest`: anchor shard o holds anchors 2048 * o to 2048 * (o + 1) - 1. The rows of one device name anchors of every one of the 8 shards, and within each of them only anchors of one aligned block of 128. The 8 anchors of a row are distinct.
All inputs are finite; a program needn't handle non-finite values.
Results may differ from the reference program's by a relative error of at most 0.0003.
Values may be sent and summed in bfloat16 or wider, within the bound.
No kernel may reach another device: no remote copies, remote signals or barrier semaphores. Data moves between devices by JAX's collectives and lax.ppermute only.
A program may use at most 128 MiB of HBM per device.

```python
import jax
import jax.numpy as jnp
from jax import lax

D = 768
COLS = 64
CAND = 8
ANC_DEV = 2048
BA = 128
ROW_DEV = 1536
OWNERS = 8
USED = 8
ANCHORS = 16384
ROWS = 49152
DEVICES = 32


def draw_nearest(key, part):
    span = USED * BA
    spacing = span // CAND
    key_order = jax.random.fold_in(key, 11)
    key_pick = jax.random.fold_in(key, 23)
    key_base = jax.random.fold_in(key, 37)
    key_jitter = jax.random.fold_in(key, 41)
    orders = jax.vmap(lambda sub_key: jax.random.permutation(sub_key, OWNERS))(jax.random.split(key_order, DEVICES))
    users = orders[:, :USED]
    picks = jax.random.randint(key_pick, (DEVICES, OWNERS), 0, ANC_DEV // BA)
    row_index = jnp.arange(ROW_DEV, dtype=jnp.int32)
    base = (row_index % USED)[None, :] * BA + jax.random.randint(key_base, (DEVICES, ROW_DEV), 0, BA)
    jitter = jax.random.randint(key_jitter, (DEVICES, ROW_DEV, CAND), 0, spacing)
    jitter = jitter * (jnp.arange(CAND, dtype=jnp.int32) > 0).astype(jnp.int32)
    places = (base[:, :, None] + jnp.arange(CAND, dtype=jnp.int32) * spacing + jitter) % span
    owner_pick = jnp.take_along_axis(users, (places // BA).reshape(DEVICES, -1), axis=1)
    block_pick = jnp.take_along_axis(picks, owner_pick, axis=1)
    anchor_ids = owner_pick * ANC_DEV + block_pick * BA + (places % BA).reshape(DEVICES, -1)
    return anchor_ids.reshape(DEVICES * ROW_DEV, CAND).astype(jnp.int32)


def block_levels(key, dims, cuts, smallest, top_value):
    factor_of, own = 1.0, jax.random.fold_in(key, 6)
    for axis_at, blocks in cuts:
        steps = jnp.exp(jax.random.uniform(jax.random.fold_in(own, axis_at), (blocks,), jnp.float32, smallest / len(cuts), top_value / len(cuts)))
        factor_of = factor_of * jnp.repeat(steps, dims[axis_at] // blocks).reshape([-1 if axis == axis_at else 1 for axis in range(len(dims))])
    return factor_of


def scatter_about(rng, shape, deviation, bound, cuts=(), held_as=jnp.bfloat16):
    values = deviation * jax.random.normal(rng, shape, jnp.float32)
    if cuts:
        values = values * block_levels(rng, shape, cuts, -0.22, 0.18)
    return jnp.clip(values, -bound, bound).astype(held_as)


def setup_inputs(seed: int = 0) -> dict:
    splits = jax.random.split(jax.random.key(seed), 5)
    return {
        "embeddings": scatter_about(splits[0], (ROWS, D), 1.0, 6.0, ((0, 32),)),
        "anchors": scatter_about(splits[1], (ANCHORS, D), 1.0, 6.0, ((0, 8),)),
        "subspace": scatter_about(splits[2], (ANCHORS, COLS), 0.5, 3.0, ((0, 8),)),
        "nearest": draw_nearest(jax.random.fold_in(splits[4], 71), 0),
    }


def reference(embeddings, anchors, subspace, nearest):
    anchor_float = anchors.astype(jnp.float32)
    anchor_scale = lax.rsqrt(lax.optimization_barrier(jnp.mean(anchor_float * anchor_float, axis=1)) + 1e-06)
    row_groups = embeddings.reshape(-1, ROW_DEV, D)
    near_groups = nearest.reshape(-1, ROW_DEV, CAND)

    def accumulate(running, inputs):
        group_rows, group_near = inputs
        rows_float = group_rows.astype(jnp.float32)
        row_scale = lax.rsqrt(lax.optimization_barrier(jnp.mean(rows_float * rows_float, axis=1)) + 1e-06)
        picked = anchor_float[group_near]
        dots = jnp.einsum('rd,rkd->rk', rows_float, picked, precision=lax.Precision.HIGHEST)
        cosine = dots * row_scale[:, None] * anchor_scale[group_near] / D
        kernel = jnp.exp((cosine - 1.0) / 0.05)
        weights = kernel / lax.optimization_barrier(jnp.sum(kernel, axis=1, keepdims=True))
        panel = subspace[group_near].astype(jnp.float32)
        projected = jnp.einsum('rk,rkc->rc', weights, panel, precision=lax.Precision.HIGHEST)
        terms = weights[:, :, None] * projected[:, None, :]
        running = running.at[group_near.reshape(-1)].add(terms.reshape(-1, COLS))
        return (running, None)
    result, _ = lax.scan(accumulate, jnp.zeros((ANCHORS, COLS), jnp.float32), (row_groups, near_groups))
    return result
```

```python
import functools
import math

import jax
import jax.numpy as jnp
from jax import lax
from jax.experimental import pallas as pl
from jax.experimental.pallas import tpu as pltpu
from jax.sharding import PartitionSpec as P

BA = 128
EPS = 1e-6
TEMPERATURE = 0.05
LANES = 128
GROUP = 2
HEADER = 8
FULL = 32704.0
STEPS_PER_OCTAVE = 256.0
MIB = 1024 * 1024

VMEM = pl.BlockSpec(memory_space=pltpu.VMEM)
SMEM = pl.BlockSpec(memory_space=pltpu.SMEM)
ANY = pl.BlockSpec(memory_space=pl.ANY)


def divide(x, by):
    if by & (by - 1) == 0:
        return lax.shift_right_logical(x, by.bit_length() - 1), x & (by - 1)
    quotient = lax.div(x, jnp.int32(by))
    return quotient, x - quotient * by


def params(limit_mib, **more):
    return pltpu.CompilerParams(vmem_limit_bytes=limit_mib * MIB, **more)


class Plan:
    def __init__(self, rows, cols):
        self.rows, self.cols = rows, cols
        self.owners = rows * cols
        self.xor = self.owners & (self.owners - 1) == 0

    def me(self):
        return lax.axis_index("arow") * self.cols + lax.axis_index("acol")

    def owner_at(self, me, step):
        return me ^ step if self.xor else lax.rem(me + step, self.owners)

    def asker_at(self, me, step):
        return me ^ step if self.xor else lax.rem(me + self.owners - step, self.owners)

    def step_of(self, me, owner):
        return me ^ owner if self.xor else lax.rem(owner - me + self.owners, self.owners)

    def pairs(self, step):
        n = self.owners
        return [(i, i ^ step if self.xor else (i - step) % n) for i in range(n)]


def prepare_kernel(plan, shard, near_ref, slot_ref, wanted_ref):
    me = plan.me()
    owner, within = divide(near_ref[...], shard)
    block, place = divide(within, BA)
    slot_ref[...] = plan.step_of(me, owner) * BA + place
    for o in range(plan.owners):
        picked = jnp.where(owner == o, block, 0)
        wanted_ref[o : o + 1, :] = jnp.full((1, LANES), jnp.max(picked), jnp.int32)


def gather_kernel(plan, depth_tiles, cols, asked_ref, anchors_ref, panel_ref, *refs):
    out, sem = refs[:-1], refs[-1]
    me = plan.me()
    copies = []
    for step in range(plan.owners):
        block = asked_ref[plan.asker_at(me, step), 0]
        start = pl.multiple_of(block * BA, BA)
        for j in range(depth_tiles):
            copies.append((
                anchors_ref.at[pl.ds(start, BA), pl.ds(j * LANES, LANES)],
                out[step].at[pl.ds(j * BA, BA), :],
            ))
        copies.append((
            panel_ref.at[:, pl.ds(start, BA)],
            out[step].at[pl.ds(depth_tiles * BA, cols), :],
        ))
    copies = [pltpu.make_async_copy(a, b, sem.at[i]) for i, (a, b) in enumerate(copies)]
    for c in copies:
        c.start()
    for c in copies:
        c.wait()


def row_scale_row(rows, depth):
    wide = rows.astype(jnp.float32)
    square = wide * wide
    high = square.astype(jnp.bfloat16)
    low = (square - high.astype(jnp.float32)).astype(jnp.bfloat16)
    ones = jnp.ones((8, depth), jnp.bfloat16)
    dims = (((1,), (1,)), ((), ()))
    total = lax.dot_general(ones, high, dims, preferred_element_type=jnp.float32)
    total += lax.dot_general(ones, low, dims, preferred_element_type=jnp.float32)
    return lax.rsqrt(total / depth + EPS)


def split(x):
    high = x.astype(jnp.bfloat16)
    return high, (x - high.astype(jnp.float32)).astype(jnp.bfloat16)


def group_body(base, depth, cols, cand, tile, messages, rows_ref, slot_ref, scale_ref, first, total_ref, high_ref, low_ref):
    depth_tiles = depth // LANES
    count = len(messages) * BA
    blocks, panels, scales = [], [], []
    for m in messages:
        block = jnp.concatenate([m[j * BA : (j + 1) * BA, :] for j in range(depth_tiles)], axis=1)
        wide = block.astype(jnp.float32)
        mean = jnp.sum(wide * wide, axis=1, keepdims=True) / depth
        scales.append(lax.rsqrt(mean + EPS) * (math.log2(math.e) / TEMPERATURE / depth))
        blocks.append(block)
        panels.append(m[depth_tiles * BA : depth_tiles * BA + cols, :])
    block = jnp.concatenate(blocks, axis=0)
    anchor_scale = jnp.concatenate(scales, axis=0)
    panel = jnp.concatenate(panels, axis=1)
    panel = jnp.concatenate([panel, jnp.ones((cols, count), jnp.bfloat16)], axis=0)
    iota = lax.broadcasted_iota(jnp.int32, (count, tile), 0) + base
    for t in range(rows_ref.shape[0] // tile):
        span = slice(t * tile, (t + 1) * tile)
        rows = rows_ref[span, :]
        if first:
            scale_ref[:, span] = row_scale_row(rows, depth)
        dots = lax.dot_general(
            block, rows, (((1,), (1,)), ((), ())), preferred_element_type=jnp.float32
        )
        hit = iota == slot_ref[0:1, span]
        for k in range(1, cand):
            hit = hit | (iota == slot_ref[k : k + 1, span])
        power = jnp.exp2(dots * anchor_scale * scale_ref[0:1, span])
        high, low = split(jnp.where(hit, power, 0.0))
        high_ref[:, span] = high
        low_ref[:, span] = low
        part = jnp.dot(panel, high, preferred_element_type=jnp.float32)
        part += jnp.dot(panel, low, preferred_element_type=jnp.float32)
        total_ref[:, span] = part if first else total_ref[:, span] + part


def first_kernel(sizes, *refs):
    n = len(refs) - 6
    messages, (rows_ref, slot_ref, scale_ref, total_ref, high_ref, low_ref) = refs[:n], refs[n:]
    group_body(0, *sizes, messages, rows_ref, slot_ref, scale_ref, True, total_ref, high_ref, low_ref)


def next_kernel(base, sizes, *refs):
    n = len(refs) - 7
    messages, (rows_ref, slot_ref, scale_ref, before_ref, total_ref, high_ref, low_ref) = refs[:n], refs[n:]
    total_ref[...] = before_ref[...]
    group_body(base, *sizes, messages, rows_ref, slot_ref, scale_ref, False, total_ref, high_ref, low_ref)


def last_kernel(plan, copies, base, sizes, n_messages, n_before, *refs):
    messages, refs = refs[:n_messages], refs[n_messages:]
    rows_ref, slot_ref, scale_ref, before_ref, wanted_ref = refs[:5]
    parts = refs[5 : 5 + 2 * n_before]
    out_ref, total, high_ref, low_ref = refs[5 + 2 * n_before :]
    cols = sizes[1]
    total[...] = before_ref[...]
    group_body(base, *sizes, messages, rows_ref, slot_ref, scale_ref, False, total, high_ref, low_ref)
    me = plan.me()
    inverse = 1.0 / total[cols : cols + 1, :]
    high, low = split(total[0:cols, :] * inverse * inverse)
    both = jnp.concatenate([high, low], axis=0)
    dims = (((1,), (1,)), ((), ()))
    step = 0
    for weights_high, weights_low in [*zip(parts[0::2], parts[1::2]), (high_ref, low_ref)]:
        main = lax.dot_general(both, weights_high[...], dims, preferred_element_type=jnp.float32)
        rest = lax.dot_general(high, weights_low[...], dims, preferred_element_type=jnp.float32)
        terms = main[:cols, :] + main[cols:, :] + rest
        for b in range(terms.shape[1] // BA):
            block = terms[:, b * BA : (b + 1) * BA]
            owner = plan.owner_at(me, step)
            top = jnp.maximum(jnp.max(jnp.abs(block), axis=0, keepdims=True), 1e-30)
            code = jnp.ceil(jnp.log2(top) * STEPS_PER_OCTAVE)
            value = jnp.round(block * (jnp.exp2(code * (-1.0 / STEPS_PER_OCTAVE)) * FULL))
            index = wanted_ref[pl.ds(owner, 1), :]
            line = lax.broadcasted_iota(jnp.int32, (HEADER, BA), 0)
            header = jnp.where(line == 0, code.astype(jnp.int32), jnp.where(line == 1, index, 0))
            message = jnp.concatenate([value.astype(jnp.int32), header], axis=0).astype(jnp.int16)
            for c in range(copies):
                out_ref[pl.ds(c * plan.owners + owner, 1)] = message[None]
            step += 1


def sum_kernel(cols, messages_ref, out_ref):
    out_ref[...] = jnp.zeros_like(out_ref)

    def add(d, carry):
        message = messages_ref[pl.ds(d, 1)][0].astype(jnp.int32)
        code = message[cols : cols + 1, :].astype(jnp.float32)
        index = jnp.max(message[cols + 1 : cols + 2, :])
        scale = jnp.exp2(code * (1.0 / STEPS_PER_OCTAVE)) * (1.0 / FULL)
        place = pl.ds(pl.multiple_of(index * BA, BA), BA)
        out_ref[:, place] += message[:cols, :].astype(jnp.float32) * scale
        return carry

    lax.fori_loop(0, messages_ref.shape[0], add, 0)


def per_device(embeddings, anchors, subspace, nearest):
    plan = Plan(lax.axis_size("arow"), lax.axis_size("acol"))
    copies = lax.axis_size("samp")
    owners = plan.owners
    shard, depth = anchors.shape
    cols = subspace.shape[1]
    rows, cand = nearest.shape
    depth_tiles = depth // LANES
    f32, bf16, i32 = jnp.float32, jnp.bfloat16, jnp.int32
    struct = jax.ShapeDtypeStruct

    slot, wanted = pl.pallas_call(
        functools.partial(prepare_kernel, plan, shard),
        out_shape=(struct((cand, rows), i32), struct((owners, LANES), i32)),
        in_specs=[VMEM],
        out_specs=(VMEM, VMEM),
        compiler_params=params(4),
        name="prepare",
    )(nearest.T)
    asked = lax.all_to_all(wanted, ("arow", "acol"), 0, 0, tiled=True)

    message = struct((depth_tiles * BA + cols, LANES), bf16)
    sent = pl.pallas_call(
        functools.partial(gather_kernel, plan, depth_tiles, cols),
        out_shape=(message,) * owners,
        in_specs=[SMEM, ANY, ANY],
        out_specs=(ANY,) * owners,
        scratch_shapes=[pltpu.SemaphoreType.DMA((owners * (depth_tiles + 1),))],
        compiler_params=params(4),
        name="gather",
    )(asked, anchors, subspace.T)
    held = [sent[0]] + [
        lax.ppermute(sent[s], ("arow", "acol"), plan.pairs(s)) for s in range(1, owners)
    ]

    tile = math.gcd(rows, 256)
    sizes = (depth, cols, cand, tile)
    size = min(GROUP, owners)
    groups = [list(range(s, min(s + size, owners))) for s in range(0, owners, size)]
    state, parts = None, []
    for g in groups[:-1]:
        n = len(g) * BA
        outs = (struct((2 * cols, rows), f32), struct((n, rows), bf16), struct((n, rows), bf16))
        cost = pl.CostEstimate(flops=2 * n * rows * (depth + 4 * cols), bytes_accessed=rows * depth * 2, transcendentals=n * rows)
        if state is None:
            scale, state, high, low = pl.pallas_call(
                functools.partial(first_kernel, sizes),
                out_shape=(struct((8, rows), f32), *outs),
                in_specs=[VMEM] * (len(g) + 2),
                out_specs=(VMEM,) * 4,
                cost_estimate=cost,
                compiler_params=params(24),
                name="first_group",
            )(*[held[s] for s in g], embeddings, slot)
        else:
            state, high, low = pl.pallas_call(
                functools.partial(next_kernel, g[0] * BA, sizes),
                out_shape=outs,
                in_specs=[VMEM] * (len(g) + 4),
                out_specs=(VMEM,) * 3,
                cost_estimate=cost,
                compiler_params=params(24),
                name="next_group",
            )(*[held[s] for s in g], embeddings, slot, scale, state)
        parts += [high, low]
    g = groups[-1]
    n = len(g) * BA
    terms = pl.pallas_call(
        functools.partial(last_kernel, plan, copies, g[0] * BA, sizes, len(g), len(parts) // 2),
        out_shape=struct((copies * owners, cols + HEADER, BA), jnp.int16),
        in_specs=[VMEM] * (len(g) + 5 + len(parts)),
        out_specs=VMEM,
        scratch_shapes=[pltpu.VMEM((2 * cols, rows), f32), pltpu.VMEM((n, rows), bf16), pltpu.VMEM((n, rows), bf16)],
        compiler_params=params(56),
        name="last_group",
    )(*[held[s] for s in g], embeddings, slot, scale, state, wanted, *parts)
    returned = lax.all_to_all(terms, ("samp", "arow", "acol"), 0, 0, tiled=True)
    result = pl.pallas_call(
        functools.partial(sum_kernel, cols),
        out_shape=struct((cols, shard), f32),
        in_specs=[VMEM],
        out_specs=VMEM,
        compiler_params=params(16),
        name="sum_terms",
    )(returned)
    return result.T


def solution(mesh):
    in_specs = (
        P(("samp", "arow", "acol"), None),
        P(("arow", "acol"), None),
        P(("arow", "acol"), None),
        P(("samp", "arow", "acol"), None),
    )
    return jax.shard_map(
        per_device, mesh=mesh, in_specs=in_specs, out_specs=P(("arow", "acol"), None), check_vma=False
    )
```

```python
import functools
import math

import jax
import jax.numpy as jnp
from jax import lax
from jax.experimental import pallas as pl
from jax.experimental.pallas import tpu as pltpu
from jax.sharding import PartitionSpec as P

BA = 128
EPS = 1e-6
TEMPERATURE = 0.05
LANES = 128
MISS = -1e30
IN_FLIGHT = 5
HEADER = 8
FULL = 32704.0
STEPS_PER_OCTAVE = 256.0
MIB = 1024 * 1024

VMEM = pl.BlockSpec(memory_space=pltpu.VMEM)
SMEM = pl.BlockSpec(memory_space=pltpu.SMEM)
ANY = pl.BlockSpec(memory_space=pl.ANY)
HBM = pl.BlockSpec(memory_space=pltpu.HBM)
QUICK = pl.CostEstimate(flops=1, bytes_accessed=1, transcendentals=0)


def divide(x, by):
    if by & (by - 1) == 0:
        return lax.shift_right_logical(x, by.bit_length() - 1), x & (by - 1)
    quotient = lax.div(x, jnp.int32(by))
    return quotient, x - quotient * by


def params(limit_mib, **more):
    return pltpu.CompilerParams(vmem_limit_bytes=int(limit_mib * MIB), **more)


class Plan:
    def __init__(self, rows, cols):
        self.rows, self.cols = rows, cols
        self.owners = rows * cols
        self.xor = self.owners & (self.owners - 1) == 0

    def me(self):
        return lax.axis_index("arow") * self.cols + lax.axis_index("acol")

    def owner_at(self, me, step):
        return me ^ step if self.xor else lax.rem(me + step, self.owners)

    def asker_at(self, me, step):
        return me ^ step if self.xor else lax.rem(me + self.owners - step, self.owners)

    def step_of(self, me, owner):
        return me ^ owner if self.xor else lax.rem(owner - me + self.owners, self.owners)

    def order(self):
        if self.owners == 8 and self.xor:
            return [(2, 0), (4, 0), (3, 0), (5, 0), (6, 0), (7, 2), (1, 4)]
        return [(s, max(s - IN_FLIGHT, 0)) for s in range(1, self.owners)]

    def sent(self):
        return [*(s for s, _ in self.order()), 0]

    def groups(self):
        if self.owners == 8 and self.xor:
            return [[0, 2], [3, 4], [1, 5], [6], [7]]
        order = list(range(1, self.owners))
        return [[0], *(order[i : min(i + 2, len(order) - 1)] for i in range(0, len(order) - 1, 2)), order[-1:]]

    def pairs(self, step):
        n = self.owners
        return [(i, i ^ step if self.xor else (i - step) % n) for i in range(n)]


def prepare_kernel(plan, shard, near_ref, slot_ref, wanted_ref):
    me = plan.me()
    owner, within = divide(near_ref[...], shard)
    block, place = divide(within, BA)
    slot_ref[...] = plan.step_of(me, owner) * BA + place
    for o in range(plan.owners):
        picked = jnp.where(owner == o, block, 0)
        wanted_ref[o : o + 1, :] = jnp.full((1, LANES), jnp.max(picked), jnp.int32)


def gather_kernel(plan, depth_tiles, cols, asked_ref, anchors_ref, panel_ref, *refs):
    out, blocks, sem = refs[:-2], refs[-2], refs[-1]
    me = plan.me()
    starts, copies, panels = {}, {}, {}
    for step in plan.sent():
        block = jnp.max(asked_ref[pl.ds(plan.asker_at(me, step), 1), :])
        starts[step] = pl.multiple_of(block * BA, BA)
        copies[step] = pltpu.make_async_copy(
            anchors_ref.at[pl.ds(starts[step], BA), :], blocks.at[step], sem.at[step]
        )
        copies[step].start()
    for step in plan.sent():
        panels[step] = pltpu.make_async_copy(
            panel_ref.at[:, pl.ds(starts[step], BA)],
            out[step].at[pl.ds(depth_tiles * BA, cols), :],
            sem.at[plan.owners + step],
        )
        panels[step].start()
    for step in plan.sent():
        copies[step].wait()
        for j in range(depth_tiles):
            out[step][j * BA : (j + 1) * BA, :] = blocks[step, :, j * LANES : (j + 1) * LANES]
    for step in plan.sent():
        panels[step].wait()


def split(x):
    high = x.astype(jnp.bfloat16)
    return high, (x - high.astype(jnp.float32)).astype(jnp.bfloat16)


def rows_kernel(rows_ref, slot_ref, turned_ref, scale_ref, bias_ref):
    rows, depth = rows_ref.shape
    tile = math.gcd(rows, 256)
    for t in range(rows // tile):
        span = slice(t * tile, (t + 1) * tile)
        turned = jnp.transpose(rows_ref[span, :])
        turned_ref[:, span] = turned
        wide = turned.astype(jnp.float32)
        mean = jnp.sum(wide * wide, axis=0, keepdims=True) / depth
        scale_ref[:, span] = jnp.broadcast_to(lax.rsqrt(mean + EPS), (8, tile))
    step, place = divide(slot_ref[...], BA)
    iota = lax.broadcasted_iota(jnp.int32, (BA, rows), 0).astype(jnp.bfloat16)
    for s in range(bias_ref.shape[0] // BA):
        key = jnp.where(step == s, place, -1).astype(jnp.bfloat16)
        bias = jnp.full(iota.shape, MISS, jnp.bfloat16)
        for k in range(slot_ref.shape[0]):
            bias = jnp.where(iota == key[k : k + 1, :], jnp.bfloat16(0), bias)
        bias_ref[s * BA : (s + 1) * BA, :] = bias


def group_body(steps, depth, cols, tile, messages, rows_ref, bias_ref, scale_ref, before, total_ref, high_ref, low_ref):
    depth_tiles = depth // LANES
    count = len(messages) * BA
    blocks, panels, scales = [], [], []
    for m in messages:
        block = jnp.concatenate([m[j * BA : (j + 1) * BA, :] for j in range(depth_tiles)], axis=1)
        wide = block.astype(jnp.float32)
        mean = jnp.sum(wide * wide, axis=1, keepdims=True) / depth
        scales.append(lax.rsqrt(mean + EPS) * (math.log2(math.e) / TEMPERATURE / depth))
        blocks.append(block)
        panels.append(m[depth_tiles * BA : depth_tiles * BA + cols, :])
    block = jnp.concatenate(blocks, axis=0)
    anchor_scale = jnp.concatenate(scales, axis=0)
    panel = jnp.concatenate(panels, axis=1)
    panel = jnp.concatenate([panel, jnp.ones((cols, count), jnp.bfloat16)], axis=0)
    for t in range(rows_ref.shape[1] // tile):
        span = slice(t * tile, (t + 1) * tile)
        dots = jnp.dot(block, rows_ref[:, span], preferred_element_type=jnp.float32)
        bias = jnp.concatenate([bias_ref[s * BA : (s + 1) * BA, span] for s in steps], axis=0)
        high, low = split(jnp.exp2(dots * anchor_scale * scale_ref[0:1, span] + bias.astype(jnp.float32)))
        high_ref[:, span] = high
        low_ref[:, span] = low
    for t in range(rows_ref.shape[1] // tile):
        span = slice(t * tile, (t + 1) * tile)
        part = jnp.dot(panel, high_ref[:, span], preferred_element_type=jnp.float32)
        part += jnp.dot(panel, low_ref[:, span], preferred_element_type=jnp.float32)
        total_ref[:, span] = part if before is None else before[:, span] + part


def group_kernel(steps, sizes, *refs):
    messages, refs = refs[: len(steps)], refs[len(steps) :]
    rows_ref, bias_ref, scale_ref = refs[:3]
    before = refs[3] if len(refs) == 7 else None
    group_body(steps, *sizes, messages, rows_ref, bias_ref, scale_ref, before, *refs[-3:])


def last_kernel(plan, copies, groups, sizes, *refs):
    steps = groups[-1]
    messages, refs = refs[: len(steps)], refs[len(steps) :]
    rows_ref, bias_ref, scale_ref, before, wanted_ref = refs[:5]
    parts = [*refs[5:-5], *refs[-3:-1]]
    out_ref, total, high_ref, low_ref, terms = refs[-5:]
    cols = sizes[1]
    group_body(steps, *sizes, messages, rows_ref, bias_ref, scale_ref, before, total, high_ref, low_ref)
    me = plan.me()
    inverse = 1.0 / total[cols : cols + 1, :]
    high, low = split(total[0:cols, :] * inverse * inverse)
    both = jnp.concatenate([high, low], axis=0)
    dims = (((1,), (1,)), ((), ()))
    at = 0
    for g, weights_high, weights_low in zip(groups, parts[0::2], parts[1::2], strict=True):
        span = slice(at, at + len(g) * BA)
        main = lax.dot_general(both, weights_high[...], dims, preferred_element_type=jnp.float32)
        rest = lax.dot_general(high, weights_low[...], dims, preferred_element_type=jnp.float32)
        terms[0 : 2 * cols, span] = main
        terms[2 * cols :, span] = rest
        at += len(g) * BA
    at = 0
    for g in groups:
        for step in g:
            span = slice(at, at + BA)
            at += BA
            block = terms[0:cols, span] + terms[cols : 2 * cols, span] + terms[2 * cols :, span]
            owner = plan.owner_at(me, step)
            top = jnp.maximum(jnp.max(jnp.abs(block), axis=0, keepdims=True), 1e-30)
            code = jnp.ceil(jnp.log2(top) * STEPS_PER_OCTAVE)
            value = jnp.round(block * (jnp.exp2(code * (-1.0 / STEPS_PER_OCTAVE)) * FULL))
            index = wanted_ref[pl.ds(owner, 1), :]
            line = lax.broadcasted_iota(jnp.int32, (HEADER, BA), 0)
            header = jnp.where(line == 0, code.astype(jnp.int32), jnp.where(line == 1, index, 0))
            message = jnp.concatenate([value.astype(jnp.int32), header], axis=0).astype(jnp.int16)
            for c in range(copies):
                out_ref[pl.ds(c * plan.owners + owner, 1)] = message[None]


def sum_kernel(cols, messages_ref, out_ref):
    out_ref[...] = jnp.zeros_like(out_ref)
    count = messages_ref.shape[0]
    batch = math.gcd(count, 32)

    def add(i, carry):
        headers = [messages_ref[i * batch + d, cols : cols + HEADER, :].astype(jnp.int32) for d in range(batch)]
        places = [pl.multiple_of(jnp.max(h[1:2, :]) * BA, BA) for h in headers]
        for d in range(batch):
            code = headers[d][0:1, :].astype(jnp.float32)
            scale = jnp.exp2(code * (1.0 / STEPS_PER_OCTAVE)) * (1.0 / FULL)
            values = messages_ref[i * batch + d, 0:cols, :].astype(jnp.int32).astype(jnp.float32)
            out_ref[:, pl.ds(places[d], BA)] += values * scale
        return carry

    lax.fori_loop(0, count // batch, add, 0, unroll=count == batch)


def per_device(embeddings, anchors, subspace, nearest):
    plan = Plan(lax.axis_size("arow"), lax.axis_size("acol"))
    copies = lax.axis_size("samp")
    owners = plan.owners
    shard, depth = anchors.shape
    cols = subspace.shape[1]
    rows, cand = nearest.shape
    depth_tiles = depth // LANES
    f32, bf16, i32 = jnp.float32, jnp.bfloat16, jnp.int32
    struct = jax.ShapeDtypeStruct

    panel = subspace.T
    slot, wanted = pl.pallas_call(
        functools.partial(prepare_kernel, plan, shard),
        out_shape=(struct((cand, rows), i32), struct((owners, LANES), i32)),
        in_specs=[VMEM],
        out_specs=(VMEM, VMEM),
        compiler_params=params(4),
        name="prepare",
    )(nearest.T)
    asked = lax.all_to_all(wanted, ("arow", "acol"), 0, 0, tiled=True)

    tile = math.gcd(rows, 256)
    message = struct((depth_tiles * BA + cols, LANES), bf16)
    sent = pl.pallas_call(
        functools.partial(gather_kernel, plan, depth_tiles, cols),
        out_shape=(message,) * owners,
        in_specs=[VMEM, HBM, HBM],
        out_specs=(VMEM,) * owners,
        scratch_shapes=[pltpu.VMEM((owners, BA, depth), bf16), pltpu.SemaphoreType.DMA((2 * owners,))],
        compiler_params=params(52.125),
        name="gather",
    )(asked, anchors, panel)
    slot, *sent = lax.optimization_barrier((slot, *sent))
    turned, scale, bias = pl.pallas_call(
        rows_kernel,
        out_shape=(struct((depth, rows), bf16), struct((8, rows), f32), struct((owners * BA, rows), bf16)),
        in_specs=[VMEM, VMEM],
        out_specs=(VMEM,) * 3,
        cost_estimate=QUICK,
        compiler_params=params(16),
        name="rows",
        )(embeddings, slot)

    sizes = (depth, cols, tile)

    def weigh(g, state):
        n = len(g) * BA
        return pl.pallas_call(
            functools.partial(group_kernel, g, sizes),
            out_shape=(struct((2 * cols, rows), f32), struct((n, rows), bf16), struct((n, rows), bf16)),
            in_specs=[VMEM] * (len(g) + 3 + len(state)),
            out_specs=(VMEM,) * 3,
            cost_estimate=QUICK,
            compiler_params=params(10),
            name="weights",
        )(*[held[s] for s in g], turned, bias, scale, *state)

    groups = plan.groups()
    held, total, parts = {0: sent[0]}, None, []
    for s, after in plan.order():
        block = sent[s]
        if after:
            block, *_ = lax.optimization_barrier((block, held[after]))
        held[s] = lax.ppermute(block, ("arow", "acol"), plan.pairs(s))
    for g in groups[:-1]:
        total, high, low = weigh(g, [] if total is None else [total])
        parts += [high, low]
    g = groups[-1]
    n = len(g) * BA
    small = owners * BA * rows * 4 <= 8 * MIB
    terms = pl.pallas_call(
        functools.partial(last_kernel, plan, copies, groups, sizes),
        out_shape=struct((copies * owners, cols + HEADER, BA), jnp.int16),
        in_specs=[VMEM] * (len(g) + 5 + len(parts)),
        out_specs=VMEM,
        cost_estimate=QUICK,
        scratch_shapes=[pltpu.VMEM((2 * cols, rows), f32), pltpu.VMEM((n, rows), bf16), pltpu.VMEM((n, rows), bf16), pltpu.VMEM((3 * cols, owners * BA), f32)],
        compiler_params=params(14 if small else 60),
        name="terms",
    )(*[held[s] for s in g], turned, bias, scale, total, wanted, *parts)
    returned = lax.all_to_all(terms, ("samp", "arow", "acol"), 0, 0, tiled=True)
    result = pl.pallas_call(
        functools.partial(sum_kernel, cols),
        out_shape=struct((cols, shard), f32),
        in_specs=[VMEM],
        out_specs=VMEM,
        compiler_params=params(16),
        name="sum_terms",
    )(returned)
    return result.T


def solution(mesh):
    in_specs = (
        P(("samp", "arow", "acol"), None),
        P(("arow", "acol"), None),
        P(("arow", "acol"), None),
        P(("samp", "arow", "acol"), None),
    )
    return jax.shard_map(
        per_device, mesh=mesh, in_specs=in_specs, out_specs=P(("arow", "acol"), None), check_vma=False
    )
```

```python
import functools
import math

import jax
import jax.numpy as jnp
from jax import lax
from jax.experimental import pallas as pl
from jax.experimental.pallas import tpu as pltpu
from jax.sharding import PartitionSpec as P

BA = 128
EPS = 1e-6
TEMPERATURE = 0.05
LANES = 128
MISS = -1e30
ORDER = [(2, 0), (4, 0), (6, 0), (3, 0), (5, 0), (7, 2), (1, 4)]
GROUPS = [[0, 2], [1, 4], [5], [3, 6], [7]]
LIMIT_EVEN, LIMIT_ODD = 52.9, 52.1
IN_FLIGHT = 5
FULL = 32704.0
STEPS_PER_OCTAVE = 256.0
MIB = 1024 * 1024

VMEM = pl.BlockSpec(memory_space=pltpu.VMEM)
SMEM = pl.BlockSpec(memory_space=pltpu.SMEM)
ANY = pl.BlockSpec(memory_space=pl.ANY)
HBM = pl.BlockSpec(memory_space=pltpu.HBM)
QUICK = pl.CostEstimate(flops=1, bytes_accessed=1, transcendentals=0)


def divide(x, by):
    if by & (by - 1) == 0:
        return lax.shift_right_logical(x, by.bit_length() - 1), x & (by - 1)
    quotient = lax.div(x, jnp.int32(by))
    return quotient, x - quotient * by


def params(limit_mib, **more):
    return pltpu.CompilerParams(vmem_limit_bytes=int(limit_mib * MIB), **more)


class Plan:
    def __init__(self, rows, cols):
        self.cols = cols
        self.owners = rows * cols
        assert self.owners & (self.owners - 1) == 0 and cols % 2 == 0

    def me(self):
        return lax.axis_index("arow") * self.cols + lax.axis_index("acol")

    def even(self):
        return list(range(0, self.owners, 2))

    def odd(self):
        return list(range(1, self.owners, 2))

    def order(self):
        if self.owners == 8:
            return ORDER
        steps = [*self.even()[1:], *self.odd()]
        return [(s, steps[i - IN_FLIGHT] if i >= IN_FLIGHT else 0) for i, s in enumerate(steps)]

    def groups(self):
        if self.owners == 8:
            return GROUPS
        order = [s for s, _ in self.order()]
        return [[0], *(order[i : min(i + 2, len(order) - 1)] for i in range(0, len(order) - 1, 2)), order[-1:]]

    def pairs(self, step):
        return [(i, i ^ step) for i in range(self.owners)]


def prepare_kernel(plan, shard, near_ref, slot_ref, wanted_ref):
    me = plan.me()
    owner, within = divide(near_ref[...], shard)
    block, place = divide(within, BA)
    slot_ref[...] = (me ^ owner) * BA + place
    for o in range(plan.owners):
        picked = jnp.where(owner == o, block, 0)
        wanted_ref[o : o + 1, :] = jnp.full((1, LANES), jnp.max(picked), jnp.int32)


def cut(starts, depth_tiles, cols, anchors_ref, panel_ref, out, blocks, sem):
    copies, panels = [], []
    for i, start in enumerate(starts):
        copies.append(pltpu.make_async_copy(anchors_ref.at[pl.ds(start, BA), :], blocks.at[i], sem.at[i]))
        copies[i].start()
    for i, start in enumerate(starts):
        panels.append(pltpu.make_async_copy(
            panel_ref.at[:, pl.ds(start, BA)], out[i].at[pl.ds(depth_tiles * BA, cols), :], sem.at[len(starts) + i]
        ))
        panels[i].start()
    for i, copy in enumerate(copies):
        copy.wait()
        for j in range(depth_tiles):
            out[i][j * BA : (j + 1) * BA, :] = blocks[i, :, j * LANES : (j + 1) * LANES]
    for panel in panels:
        panel.wait()


def block_start(line):
    return pl.multiple_of(jnp.max(line) * BA, BA)


def even_kernel(plan, depth_tiles, cols, *refs):
    n = len(plan.even())
    asked, (anchors_ref, panel_ref), out = refs[:n], refs[n : n + 2], refs[n + 2 : 2 * n + 2]
    passed_ref, blocks, sem = refs[2 * n + 2 :]
    me = plan.me()
    starts = [block_start(a[pl.ds(me, 1), :]) for a in asked]
    passed_ref[...] = jnp.zeros_like(passed_ref)
    for i, a in enumerate(asked):
        passed_ref[i : i + 1, :] = a[pl.ds(me ^ 1, 1), :]
    cut(starts, depth_tiles, cols, anchors_ref, panel_ref, out, blocks, sem)


def odd_kernel(plan, depth_tiles, cols, passed_ref, anchors_ref, panel_ref, *refs):
    n = len(plan.odd())
    starts = [block_start(passed_ref[i : i + 1, :]) for i in range(n)]
    cut(starts, depth_tiles, cols, anchors_ref, panel_ref, refs[:n], *refs[n:])


def split(x):
    high = x.astype(jnp.bfloat16)
    return high, (x - high.astype(jnp.float32)).astype(jnp.bfloat16)


def rows_kernel(rows_ref, slot_ref, turned_ref, scale_ref, bias_ref):
    rows, depth = rows_ref.shape
    tile = math.gcd(rows, 256)
    for t in range(rows // tile):
        span = slice(t * tile, (t + 1) * tile)
        turned = jnp.transpose(rows_ref[span, :])
        turned_ref[:, span] = turned
        wide = turned.astype(jnp.float32)
        mean = jnp.sum(wide * wide, axis=0, keepdims=True) / depth
        scale_ref[:, span] = jnp.broadcast_to(lax.rsqrt(mean + EPS), (8, tile))
    step, place = divide(slot_ref[...], BA)
    iota = lax.broadcasted_iota(jnp.int32, (BA, rows), 0).astype(jnp.bfloat16)
    for s in range(bias_ref.shape[0] // BA):
        key = jnp.where(step == s, place, -1).astype(jnp.bfloat16)
        bias = jnp.full(iota.shape, MISS, jnp.bfloat16)
        for k in range(slot_ref.shape[0]):
            bias = jnp.where(iota == key[k : k + 1, :], jnp.bfloat16(0), bias)
        bias_ref[s * BA : (s + 1) * BA, :] = bias


def group_body(steps, depth, cols, tile, messages, rows_ref, bias_ref, scale_ref, before, total_ref, high_ref, low_ref):
    depth_tiles = depth // LANES
    count = len(messages) * BA
    blocks, panels, scales = [], [], []
    for m in messages:
        block = jnp.concatenate([m[j * BA : (j + 1) * BA, :] for j in range(depth_tiles)], axis=1)
        wide = block.astype(jnp.float32)
        mean = jnp.sum(wide * wide, axis=1, keepdims=True) / depth
        scales.append(lax.rsqrt(mean + EPS) * (math.log2(math.e) / TEMPERATURE / depth))
        blocks.append(block)
        panels.append(m[depth_tiles * BA : depth_tiles * BA + cols, :])
    block = jnp.concatenate(blocks, axis=0)
    anchor_scale = jnp.concatenate(scales, axis=0)
    panel = jnp.concatenate(panels, axis=1)
    panel = jnp.concatenate([panel, jnp.ones((cols, count), jnp.bfloat16)], axis=0)
    for t in range(rows_ref.shape[1] // tile):
        span = slice(t * tile, (t + 1) * tile)
        dots = jnp.dot(block, rows_ref[:, span], preferred_element_type=jnp.float32)
        bias = jnp.concatenate([bias_ref[s * BA : (s + 1) * BA, span] for s in steps], axis=0)
        high, low = split(jnp.exp2(dots * anchor_scale * scale_ref[0:1, span] + bias.astype(jnp.float32)))
        high_ref[:, span] = high
        low_ref[:, span] = low
    for t in range(rows_ref.shape[1] // tile):
        span = slice(t * tile, (t + 1) * tile)
        part = jnp.dot(panel, high_ref[:, span], preferred_element_type=jnp.float32)
        part += jnp.dot(panel, low_ref[:, span], preferred_element_type=jnp.float32)
        total_ref[:, span] = part if before is None else before[:, span] + part


def group_kernel(steps, sizes, *refs):
    messages, refs = refs[: len(steps)], refs[len(steps) :]
    rows_ref, bias_ref, scale_ref = refs[:3]
    before = refs[3] if len(refs) == 7 else None
    group_body(steps, *sizes, messages, rows_ref, bias_ref, scale_ref, before, *refs[-3:])


def last_kernel(plan, copies, groups, sizes, *refs):
    steps = groups[-1]
    messages, refs = refs[: len(steps)], refs[len(steps) :]
    rows_ref, bias_ref, scale_ref, before, wanted_ref = refs[:5]
    parts = [*refs[5:-5], *refs[-3:-1]]
    out_ref, total, high_ref, low_ref, terms = refs[-5:]
    cols = sizes[1]
    group_body(steps, *sizes, messages, rows_ref, bias_ref, scale_ref, before, total, high_ref, low_ref)
    me = plan.me()
    inverse = 1.0 / total[cols : cols + 1, :]
    high, low = split(total[0:cols, :] * inverse * inverse)
    both = jnp.concatenate([high, low], axis=0)
    dims = (((1,), (1,)), ((), ()))
    for g, weights_high, weights_low in zip(groups, parts[0::2], parts[1::2], strict=True):
        main = lax.dot_general(both, weights_high[...], dims, preferred_element_type=jnp.float32)
        rest = lax.dot_general(high, weights_low[...], dims, preferred_element_type=jnp.float32)
        for b, step in enumerate(g):
            span, to = slice(b * BA, (b + 1) * BA), slice(step * BA, (step + 1) * BA)
            terms[:, to] = main[:cols, span] + main[cols:, span] + rest[:, span]
    size = cols // 2 + 1
    for owner in range(plan.owners):
        block = terms[:, pl.ds(pl.multiple_of((me ^ owner) * BA, BA), BA)]
        top = jnp.maximum(jnp.max(jnp.abs(block), axis=0, keepdims=True), 1e-30)
        code = jnp.ceil(jnp.log2(top) * STEPS_PER_OCTAVE)
        value = jnp.round(block * (jnp.exp2(code * (-1.0 / STEPS_PER_OCTAVE)) * FULL)).astype(jnp.int32)
        pairs = jnp.left_shift(value[: cols // 2, :], 16) | (value[cols // 2 :, :] & 0xFFFF)
        header = jnp.left_shift(code.astype(jnp.int32), 16) | wanted_ref[owner : owner + 1, :]
        message = jnp.concatenate([pairs, header], axis=0)
        for c in range(copies):
            at = (c * plan.owners + owner) * size
            out_ref[at : at + size, :] = message


def sum_kernel(cols, messages_ref, out_ref):
    out_ref[...] = jnp.zeros_like(out_ref)
    half = cols // 2
    size = half + 1
    count = messages_ref.shape[0] // size
    batch = math.gcd(count, 32)

    def add(i, carry):
        part = messages_ref.at[pl.ds(pl.multiple_of(i * batch * size, 8), batch * size), :]
        headers = [part[d * size + half : (d + 1) * size, :] for d in range(batch)]
        places = [pl.multiple_of(jnp.max(h & 0xFFFF) * BA, BA) for h in headers]
        for d in range(batch):
            code = jnp.right_shift(headers[d], 16).astype(jnp.float32)
            scale = jnp.exp2(code * (1.0 / STEPS_PER_OCTAVE)) * (1.0 / FULL)
            pairs = part[d * size : d * size + half, :]
            first = jnp.right_shift(pairs, 16).astype(jnp.float32)
            second = jnp.right_shift(jnp.left_shift(pairs, 16), 16).astype(jnp.float32)
            out_ref[:half, pl.ds(places[d], BA)] += first * scale
            out_ref[half:, pl.ds(places[d], BA)] += second * scale
        return carry

    lax.fori_loop(0, count // batch, add, 0, unroll=count == batch)


def per_device(embeddings, anchors, subspace, nearest):
    plan = Plan(lax.axis_size("arow"), lax.axis_size("acol"))
    copies = lax.axis_size("samp")
    owners = plan.owners
    shard, depth = anchors.shape
    cols = subspace.shape[1]
    rows, cand = nearest.shape
    depth_tiles = depth // LANES
    f32, bf16, i32 = jnp.float32, jnp.bfloat16, jnp.int32
    struct = jax.ShapeDtypeStruct

    panel = subspace.T
    slot, wanted = pl.pallas_call(
        functools.partial(prepare_kernel, plan, shard),
        out_shape=(struct((cand, rows), i32), struct((owners, LANES), i32)),
        in_specs=[VMEM],
        out_specs=(VMEM, VMEM),
        compiler_params=params(4),
        name="prepare",
    )(nearest.T)
    here = ("arow", "acol")
    tile = math.gcd(rows, 256)

    message = struct((depth_tiles * BA + cols, LANES), bf16)
    even, odd = plan.even(), plan.odd()
    half = len(even)
    scratch = [pltpu.VMEM((half, BA, depth), bf16), pltpu.SemaphoreType.DMA((2 * half,))]
    passed = struct((-(-half // 8) * 8, LANES), i32)
    asked = [wanted, *(lax.ppermute(wanted, here, plan.pairs(s)) for s in even[1:])]
    *sent_even, passed = pl.pallas_call(
        functools.partial(even_kernel, plan, depth_tiles, cols),
        out_shape=(*(message,) * half, passed),
        in_specs=[*[VMEM] * half, HBM, HBM],
        out_specs=(VMEM,) * (half + 1),
        scratch_shapes=scratch,
        cost_estimate=QUICK,
        compiler_params=params(LIMIT_EVEN),
        name="cut_even",
    )(*asked, anchors, panel)
    passed = lax.ppermute(passed, here, plan.pairs(1))
    sent_odd = pl.pallas_call(
        functools.partial(odd_kernel, plan, depth_tiles, cols),
        out_shape=(message,) * half,
        in_specs=[VMEM, HBM, HBM],
        out_specs=(VMEM,) * half,
        scratch_shapes=scratch,
        cost_estimate=QUICK,
        compiler_params=params(LIMIT_ODD),
        name="cut_odd",
    )(passed, anchors, panel)
    slot, *sent_odd = lax.optimization_barrier((slot, *sent_odd))
    sent = {**dict(zip(even, sent_even)), **dict(zip(odd, sent_odd))}
    turned, scale, bias = pl.pallas_call(
        rows_kernel,
        out_shape=(struct((depth, rows), bf16), struct((8, rows), f32), struct((owners * BA, rows), bf16)),
        in_specs=[VMEM, VMEM],
        out_specs=(VMEM,) * 3,
        cost_estimate=QUICK,
        compiler_params=params(16),
        name="rows",
        )(embeddings, slot)

    sizes = (depth, cols, tile)

    def weigh(g, state):
        n = len(g) * BA
        return pl.pallas_call(
            functools.partial(group_kernel, g, sizes),
            out_shape=(struct((2 * cols, rows), f32), struct((n, rows), bf16), struct((n, rows), bf16)),
            in_specs=[VMEM] * (len(g) + 3 + len(state)),
            out_specs=(VMEM,) * 3,
            cost_estimate=QUICK,
            compiler_params=params(10),
            name="weights",
        )(*[held[s] for s in g], turned, bias, scale, *state)

    groups = plan.groups()
    held, total, parts = {0: sent[0]}, None, []
    for s, after in plan.order():
        block = sent[s]
        if after:
            block, *_ = lax.optimization_barrier((block, held[after]))
        held[s] = lax.ppermute(block, here, plan.pairs(s))
    for g in groups[:-1]:
        total, high, low = weigh(g, [] if total is None else [total])
        parts += [high, low]
    g = groups[-1]
    n = len(g) * BA
    small = owners * BA * rows * 4 <= 8 * MIB
    terms = pl.pallas_call(
        functools.partial(last_kernel, plan, copies, groups, sizes),
        out_shape=struct((copies * owners * (cols // 2 + 1), BA), i32),
        in_specs=[VMEM] * (len(g) + 5 + len(parts)),
        out_specs=VMEM,
        cost_estimate=QUICK,
        scratch_shapes=[pltpu.VMEM((2 * cols, rows), f32), pltpu.VMEM((n, rows), bf16), pltpu.VMEM((n, rows), bf16), pltpu.VMEM((cols, owners * BA), f32)],
        compiler_params=params(14 if small else 60),
        name="terms",
    )(*[held[s] for s in g], turned, bias, scale, total, wanted, *parts)
    returned = lax.all_to_all(terms[:, None, :], ("samp", "arow", "acol"), 0, 0, tiled=True)[:, 0, :]
    result = pl.pallas_call(
        functools.partial(sum_kernel, cols),
        out_shape=struct((cols, shard), f32),
        in_specs=[VMEM],
        out_specs=VMEM,
        compiler_params=params(16),
        name="sum_terms",
    )(returned)
    return result.T


def solution(mesh):
    in_specs = (
        P(("samp", "arow", "acol"), None),
        P(("arow", "acol"), None),
        P(("arow", "acol"), None),
        P(("samp", "arow", "acol"), None),
    )
    return jax.shard_map(
        per_device, mesh=mesh, in_specs=in_specs, out_specs=P(("arow", "acol"), None), check_vma=False
    )
```

```python
import functools
import math

import jax
import jax.numpy as jnp
from jax import lax
from jax.experimental import pallas as pl
from jax.experimental.pallas import tpu as pltpu
from jax.sharding import PartitionSpec as P

BA = 128
EPS = 1e-6
TEMPERATURE = 0.05
LANES = 128
MISS = -1e30
ORDER = [(2, 0), (4, 0), (6, 0), (3, 0), (5, 0), (7, 2), (1, 4)]
GROUPS = [[0, 2], [1, 4], [5], [3, 6], [7]]
LIMIT_STAGE = 49
IN_FLIGHT = 5
FULL = 32704.0
STEPS_PER_OCTAVE = 256.0
MIB = 1024 * 1024

VMEM = pl.BlockSpec(memory_space=pltpu.VMEM)
SMEM = pl.BlockSpec(memory_space=pltpu.SMEM)
ANY = pl.BlockSpec(memory_space=pl.ANY)
HBM = pl.BlockSpec(memory_space=pltpu.HBM)
QUICK = pl.CostEstimate(flops=1, bytes_accessed=1, transcendentals=0)


def divide(x, by):
    if by & (by - 1) == 0:
        return lax.shift_right_logical(x, by.bit_length() - 1), x & (by - 1)
    quotient = lax.div(x, jnp.int32(by))
    return quotient, x - quotient * by


def params(limit_mib, **more):
    return pltpu.CompilerParams(vmem_limit_bytes=int(limit_mib * MIB), **more)


class Plan:
    def __init__(self, rows, cols):
        self.cols = cols
        self.owners = rows * cols
        assert self.owners & (self.owners - 1) == 0 and cols % 2 == 0

    def me(self):
        return lax.axis_index("arow") * self.cols + lax.axis_index("acol")

    def even(self):
        return [0, *range(self.owners - 2, 0, -2)]

    def odd(self):
        return list(range(1, self.owners, 2))

    def order(self):
        if self.owners == 8:
            return ORDER
        steps = [*self.even()[:0:-1], *self.odd()]
        return [(s, steps[i - IN_FLIGHT] if i >= IN_FLIGHT else 0) for i, s in enumerate(steps)]

    def groups(self):
        if self.owners == 8:
            return GROUPS
        order = [s for s, _ in self.order()]
        return [[0], *(order[i : min(i + 2, len(order) - 1)] for i in range(0, len(order) - 1, 2)), order[-1:]]

    def pairs(self, step):
        return [(i, i ^ step) for i in range(self.owners)]


def prepare_kernel(plan, shard, near_ref, slot_ref, wanted_ref):
    me = plan.me()
    owner, within = divide(near_ref[...], shard)
    block, place = divide(within, BA)
    slot_ref[...] = (me ^ owner) * BA + place
    for o in range(plan.owners):
        picked = jnp.where(owner == o, block, 0)
        wanted_ref[o : o + 1, :] = jnp.full((1, LANES), jnp.max(picked), jnp.int32)


def stage_kernel(_, anchors_ref, panel_ref, anchors_out, panel_out, sem):
    copies = [
        pltpu.make_async_copy(anchors_ref, anchors_out, sem.at[0]),
        pltpu.make_async_copy(panel_ref, panel_out, sem.at[1]),
    ]
    for copy in copies:
        copy.start()
    for copy in copies:
        copy.wait()


def cut(starts, depth_tiles, cols, anchors_ref, panel_ref, out):
    for i, start in enumerate(starts):
        for j in range(depth_tiles):
            out[i][j * BA : (j + 1) * BA, :] = anchors_ref[pl.ds(start, BA), j * LANES : (j + 1) * LANES]
        out[i][depth_tiles * BA :, :] = panel_ref[:, pl.ds(start, BA)]


def block_start(line):
    return pl.multiple_of(jnp.max(line) * BA, BA)


def even_kernel(plan, depth_tiles, cols, *refs):
    n = len(plan.even())
    asked, (anchors_ref, panel_ref), out = refs[:n], refs[n : n + 2], refs[n + 2 : 2 * n + 2]
    passed_ref = refs[2 * n + 2]
    me = plan.me()
    starts = [block_start(a[pl.ds(me, 1), :]) for a in asked]
    passed_ref[...] = jnp.zeros_like(passed_ref)
    for s, a in zip(plan.even(), asked):
        passed_ref[s // 2 : s // 2 + 1, :] = a[pl.ds(me ^ 1, 1), :]
    cut(starts, depth_tiles, cols, anchors_ref, panel_ref, out)


def odd_kernel(plan, depth_tiles, cols, passed_ref, anchors_ref, panel_ref, *refs):
    n = len(plan.odd())
    starts = [block_start(passed_ref[i : i + 1, :]) for i in range(n)]
    cut(starts, depth_tiles, cols, anchors_ref, panel_ref, refs)


def split(x):
    high = x.astype(jnp.bfloat16)
    return high, (x - high.astype(jnp.float32)).astype(jnp.bfloat16)


def rows_kernel(rows_ref, slot_ref, turned_ref, scale_ref, bias_ref):
    rows, depth = rows_ref.shape
    tile = math.gcd(rows, 256)
    for t in range(rows // tile):
        span = slice(t * tile, (t + 1) * tile)
        turned = jnp.transpose(rows_ref[span, :])
        turned_ref[:, span] = turned
        wide = turned.astype(jnp.float32)
        mean = jnp.sum(wide * wide, axis=0, keepdims=True) / depth
        scale_ref[:, span] = jnp.broadcast_to(lax.rsqrt(mean + EPS), (8, tile))
    step, place = divide(slot_ref[...], BA)
    iota = lax.broadcasted_iota(jnp.int32, (BA, rows), 0).astype(jnp.bfloat16)
    for s in range(bias_ref.shape[0] // BA):
        key = jnp.where(step == s, place, -1).astype(jnp.bfloat16)
        bias = jnp.full(iota.shape, MISS, jnp.bfloat16)
        for k in range(slot_ref.shape[0]):
            bias = jnp.where(iota == key[k : k + 1, :], jnp.bfloat16(0), bias)
        bias_ref[s * BA : (s + 1) * BA, :] = bias


def group_body(steps, depth, cols, tile, messages, rows_ref, bias_ref, scale_ref, before, total_ref, high_ref, low_ref):
    depth_tiles = depth // LANES
    count = len(messages) * BA
    blocks, panels, scales = [], [], []
    for m in messages:
        block = jnp.concatenate([m[j * BA : (j + 1) * BA, :] for j in range(depth_tiles)], axis=1)
        wide = block.astype(jnp.float32)
        mean = jnp.sum(wide * wide, axis=1, keepdims=True) / depth
        scales.append(lax.rsqrt(mean + EPS) * (math.log2(math.e) / TEMPERATURE / depth))
        blocks.append(block)
        panels.append(m[depth_tiles * BA : depth_tiles * BA + cols, :])
    block = jnp.concatenate(blocks, axis=0)
    anchor_scale = jnp.concatenate(scales, axis=0)
    panel = jnp.concatenate(panels, axis=1)
    panel = jnp.concatenate([panel, jnp.ones((cols, count), jnp.bfloat16)], axis=0)
    for t in range(rows_ref.shape[1] // tile):
        span = slice(t * tile, (t + 1) * tile)
        dots = jnp.dot(block, rows_ref[:, span], preferred_element_type=jnp.float32)
        bias = jnp.concatenate([bias_ref[s * BA : (s + 1) * BA, span] for s in steps], axis=0)
        high, low = split(jnp.exp2(dots * anchor_scale * scale_ref[0:1, span] + bias.astype(jnp.float32)))
        high_ref[:, span] = high
        low_ref[:, span] = low
    for t in range(rows_ref.shape[1] // tile):
        span = slice(t * tile, (t + 1) * tile)
        part = jnp.dot(panel, high_ref[:, span], preferred_element_type=jnp.float32)
        part += jnp.dot(panel, low_ref[:, span], preferred_element_type=jnp.float32)
        total_ref[:, span] = part if before is None else before[:, span] + part


def group_kernel(steps, sizes, *refs):
    messages, refs = refs[: len(steps)], refs[len(steps) :]
    rows_ref, bias_ref, scale_ref = refs[:3]
    before = refs[3] if len(refs) == 7 else None
    group_body(steps, *sizes, messages, rows_ref, bias_ref, scale_ref, before, *refs[-3:])


def last_kernel(plan, copies, groups, sizes, *refs):
    steps = groups[-1]
    messages, refs = refs[: len(steps)], refs[len(steps) :]
    rows_ref, bias_ref, scale_ref, before, wanted_ref = refs[:5]
    parts = [*refs[5:-5], *refs[-3:-1]]
    out_ref, total, high_ref, low_ref, terms = refs[-5:]
    cols = sizes[1]
    group_body(steps, *sizes, messages, rows_ref, bias_ref, scale_ref, before, total, high_ref, low_ref)
    me = plan.me()
    inverse = 1.0 / total[cols : cols + 1, :]
    high, low = split(total[0:cols, :] * inverse * inverse)
    both = jnp.concatenate([high, low], axis=0)
    dims = (((1,), (1,)), ((), ()))
    for g, weights_high, weights_low in zip(groups, parts[0::2], parts[1::2], strict=True):
        main = lax.dot_general(both, weights_high[...], dims, preferred_element_type=jnp.float32)
        rest = lax.dot_general(high, weights_low[...], dims, preferred_element_type=jnp.float32)
        for b, step in enumerate(g):
            span, to = slice(b * BA, (b + 1) * BA), slice(step * BA, (step + 1) * BA)
            terms[:, to] = main[:cols, span] + main[cols:, span] + rest[:, span]
    size = cols // 2 + 1
    for owner in range(plan.owners):
        block = terms[:, pl.ds(pl.multiple_of((me ^ owner) * BA, BA), BA)]
        top = jnp.maximum(jnp.max(jnp.abs(block), axis=0, keepdims=True), 1e-30)
        code = jnp.ceil(jnp.log2(top) * STEPS_PER_OCTAVE)
        value = jnp.round(block * (jnp.exp2(code * (-1.0 / STEPS_PER_OCTAVE)) * FULL)).astype(jnp.int32)
        pairs = jnp.left_shift(value[: cols // 2, :], 16) | (value[cols // 2 :, :] & 0xFFFF)
        header = jnp.left_shift(code.astype(jnp.int32), 16) | wanted_ref[owner : owner + 1, :]
        message = jnp.concatenate([pairs, header], axis=0)
        for c in range(copies):
            at = (c * plan.owners + owner) * size
            out_ref[at : at + size, :] = message


def sum_kernel(cols, messages_ref, out_ref):
    out_ref[...] = jnp.zeros_like(out_ref)
    half = cols // 2
    size = half + 1
    count = messages_ref.shape[0] // size
    batch = math.gcd(count, 32)

    def add(i, carry):
        part = messages_ref.at[pl.ds(pl.multiple_of(i * batch * size, 8), batch * size), :]
        headers = [part[d * size + half : (d + 1) * size, :] for d in range(batch)]
        places = [pl.multiple_of(jnp.max(h & 0xFFFF) * BA, BA) for h in headers]
        for d in range(batch):
            code = jnp.right_shift(headers[d], 16).astype(jnp.float32)
            scale = jnp.exp2(code * (1.0 / STEPS_PER_OCTAVE)) * (1.0 / FULL)
            pairs = part[d * size : d * size + half, :]
            first = jnp.right_shift(pairs, 16).astype(jnp.float32)
            second = jnp.right_shift(jnp.left_shift(pairs, 16), 16).astype(jnp.float32)
            out_ref[:half, pl.ds(places[d], BA)] += first * scale
            out_ref[half:, pl.ds(places[d], BA)] += second * scale
        return carry

    lax.fori_loop(0, count // batch, add, 0, unroll=count == batch)


def per_device(embeddings, anchors, subspace, nearest):
    plan = Plan(lax.axis_size("arow"), lax.axis_size("acol"))
    copies = lax.axis_size("samp")
    owners = plan.owners
    shard, depth = anchors.shape
    cols = subspace.shape[1]
    rows, cand = nearest.shape
    depth_tiles = depth // LANES
    f32, bf16, i32 = jnp.float32, jnp.bfloat16, jnp.int32
    struct = jax.ShapeDtypeStruct

    panel = subspace.T
    slot, wanted = pl.pallas_call(
        functools.partial(prepare_kernel, plan, shard),
        out_shape=(struct((cand, rows), i32), struct((owners, LANES), i32)),
        in_specs=[VMEM],
        out_specs=(VMEM, VMEM),
        compiler_params=params(4),
        name="prepare",
    )(nearest.T)
    here = ("arow", "acol")
    tile = math.gcd(rows, 256)

    message = struct((depth_tiles * BA + cols, LANES), bf16)
    even, odd = plan.even(), plan.odd()
    half = len(even)
    staged = pl.pallas_call(
        stage_kernel,
        out_shape=(struct(anchors.shape, bf16), struct(panel.shape, bf16)),
        in_specs=[VMEM, HBM, HBM],
        out_specs=(VMEM, VMEM),
        scratch_shapes=[pltpu.SemaphoreType.DMA((2,))],
        cost_estimate=QUICK,
        compiler_params=params(LIMIT_STAGE),
        name="stage",
    )(wanted, anchors, panel)
    passed = struct((-(-half // 8) * 8, LANES), i32)
    asked = [wanted, *(lax.ppermute(wanted, here, plan.pairs(s)) for s in even[1:])]
    *sent_even, passed = pl.pallas_call(
        functools.partial(even_kernel, plan, depth_tiles, cols),
        out_shape=(*(message,) * half, passed),
        in_specs=[VMEM] * (half + 2),
        out_specs=(VMEM,) * (half + 1),
        cost_estimate=QUICK,
        compiler_params=params(4),
        name="cut_even",
    )(*asked, *staged)
    passed = lax.ppermute(passed, here, plan.pairs(1))
    sent_odd = pl.pallas_call(
        functools.partial(odd_kernel, plan, depth_tiles, cols),
        out_shape=(message,) * half,
        in_specs=[VMEM] * 3,
        out_specs=(VMEM,) * half,
        cost_estimate=QUICK,
        compiler_params=params(4),
        name="cut_odd",
    )(passed, *staged)
    slot, *sent_odd = lax.optimization_barrier((slot, *sent_odd))
    sent = {**dict(zip(even, sent_even)), **dict(zip(odd, sent_odd))}
    turned, scale, bias = pl.pallas_call(
        rows_kernel,
        out_shape=(struct((depth, rows), bf16), struct((8, rows), f32), struct((owners * BA, rows), bf16)),
        in_specs=[VMEM, VMEM],
        out_specs=(VMEM,) * 3,
        cost_estimate=QUICK,
        compiler_params=params(16),
        name="rows",
        )(embeddings, slot)

    sizes = (depth, cols, tile)

    def weigh(g, state):
        n = len(g) * BA
        return pl.pallas_call(
            functools.partial(group_kernel, g, sizes),
            out_shape=(struct((2 * cols, rows), f32), struct((n, rows), bf16), struct((n, rows), bf16)),
            in_specs=[VMEM] * (len(g) + 3 + len(state)),
            out_specs=(VMEM,) * 3,
            cost_estimate=QUICK,
            compiler_params=params(10),
            name="weights",
        )(*[held[s] for s in g], turned, bias, scale, *state)

    groups = plan.groups()
    held, total, parts = {0: sent[0]}, None, []
    for s, after in plan.order():
        block = sent[s]
        if after:
            block, *_ = lax.optimization_barrier((block, held[after]))
        held[s] = lax.ppermute(block, here, plan.pairs(s))
    for g in groups[:-1]:
        total, high, low = weigh(g, [] if total is None else [total])
        parts += [high, low]
    g = groups[-1]
    n = len(g) * BA
    small = owners * BA * rows * 4 <= 8 * MIB
    terms = pl.pallas_call(
        functools.partial(last_kernel, plan, copies, groups, sizes),
        out_shape=struct((copies * owners * (cols // 2 + 1), BA), i32),
        in_specs=[VMEM] * (len(g) + 5 + len(parts)),
        out_specs=VMEM,
        cost_estimate=QUICK,
        scratch_shapes=[pltpu.VMEM((2 * cols, rows), f32), pltpu.VMEM((n, rows), bf16), pltpu.VMEM((n, rows), bf16), pltpu.VMEM((cols, owners * BA), f32)],
        compiler_params=params(14 if small else 60),
        name="terms",
    )(*[held[s] for s in g], turned, bias, scale, total, wanted, *parts)
    returned = lax.all_to_all(terms[:, None, :], ("samp", "arow", "acol"), 0, 0, tiled=True)[:, 0, :]
    result = pl.pallas_call(
        functools.partial(sum_kernel, cols),
        out_shape=struct((cols, shard), f32),
        in_specs=[VMEM],
        out_specs=VMEM,
        compiler_params=params(16),
        name="sum_terms",
    )(returned)
    return result.T


def solution(mesh):
    in_specs = (
        P(("samp", "arow", "acol"), None),
        P(("arow", "acol"), None),
        P(("arow", "acol"), None),
        P(("samp", "arow", "acol"), None),
    )
    return jax.shard_map(
        per_device, mesh=mesh, in_specs=in_specs, out_specs=P(("arow", "acol"), None), check_vma=False
    )
```

```python
import functools
import math

import jax
import jax.numpy as jnp
from jax import lax
from jax.experimental import pallas as pl
from jax.experimental.pallas import tpu as pltpu
from jax.sharding import PartitionSpec as P

BA = 128
EPS = 1e-6
TEMPERATURE = 0.05
LANES = 128
MISS = -1e30
ORDER = [(2, 0), (4, 0), (6, 0), (3, 0), (5, 0), (7, 2), (1, 4)]
GROUPS = [[0, 2], [1, 4], [5], [3, 6], [7]]
LIMIT_STAGE = 49
IN_FLIGHT = 5
FULL = 32704.0
STEPS_PER_OCTAVE = 256.0
MIB = 1024 * 1024

VMEM = pl.BlockSpec(memory_space=pltpu.VMEM)
SMEM = pl.BlockSpec(memory_space=pltpu.SMEM)
ANY = pl.BlockSpec(memory_space=pl.ANY)
HBM = pl.BlockSpec(memory_space=pltpu.HBM)
QUICK = pl.CostEstimate(flops=1, bytes_accessed=1, transcendentals=0)


def divide(x, by):
    if by & (by - 1) == 0:
        return lax.shift_right_logical(x, by.bit_length() - 1), x & (by - 1)
    quotient = lax.div(x, jnp.int32(by))
    return quotient, x - quotient * by


def params(limit_mib, **more):
    return pltpu.CompilerParams(vmem_limit_bytes=int(limit_mib * MIB), **more)


class Plan:
    def __init__(self, rows, cols):
        self.cols = cols
        self.owners = rows * cols
        assert self.owners & (self.owners - 1) == 0 and cols % 2 == 0

    def me(self):
        return lax.axis_index("arow") * self.cols + lax.axis_index("acol")

    def even(self):
        return [0, *range(self.owners - 2, 0, -2)]

    def odd(self):
        return list(range(1, self.owners, 2))

    def order(self):
        if self.owners == 8:
            return ORDER
        steps = [*self.even()[:0:-1], *self.odd()]
        return [(s, steps[i - IN_FLIGHT] if i >= IN_FLIGHT else 0) for i, s in enumerate(steps)]

    def groups(self):
        if self.owners == 8:
            return GROUPS
        order = [s for s, _ in self.order()]
        return [[0], *(order[i : min(i + 2, len(order) - 1)] for i in range(0, len(order) - 1, 2)), order[-1:]]

    def pairs(self, step):
        return [(i, i ^ step) for i in range(self.owners)]


def prepare_kernel(plan, shard, near_ref, slot_ref, wanted_ref):
    me = plan.me()
    owner, within = divide(near_ref[...], shard)
    block, place = divide(within, BA)
    slot_ref[...] = (me ^ owner) * BA + place
    for o in range(plan.owners):
        picked = jnp.where(owner == o, block, 0)
        wanted_ref[o : o + 1, :] = jnp.full((1, LANES), jnp.max(picked), jnp.int32)


def stage_kernel(_, anchors_ref, panel_ref, anchors_out, panel_out, sem):
    copies = [
        pltpu.make_async_copy(anchors_ref, anchors_out, sem.at[0]),
        pltpu.make_async_copy(panel_ref, panel_out, sem.at[1]),
    ]
    for copy in copies:
        copy.start()
    for copy in copies:
        copy.wait()


def cut(starts, depth_tiles, cols, anchors_ref, panel_ref, out):
    for i, start in enumerate(starts):
        for j in range(depth_tiles):
            out[i][j * BA : (j + 1) * BA, :] = anchors_ref[pl.ds(start, BA), j * LANES : (j + 1) * LANES]
        out[i][depth_tiles * BA :, :] = panel_ref[:, pl.ds(start, BA)]


def block_start(line):
    return pl.multiple_of(line[0, 0] * BA, BA)


def even_kernel(plan, depth_tiles, cols, *refs):
    n = len(plan.even())
    asked, (anchors_ref, panel_ref), out = refs[:n], refs[n : n + 2], refs[n + 2 : 2 * n + 2]
    passed_ref = refs[2 * n + 2]
    me = plan.me()
    starts = [block_start(a[pl.ds(me, 1), :]) for a in asked]
    passed_ref[...] = jnp.zeros_like(passed_ref)
    for s, a in zip(plan.even(), asked):
        passed_ref[s // 2 : s // 2 + 1, :] = a[pl.ds(me ^ 1, 1), :]
    cut(starts, depth_tiles, cols, anchors_ref, panel_ref, out)


def odd_kernel(plan, depth_tiles, cols, passed_ref, anchors_ref, panel_ref, *refs):
    n = len(plan.odd())
    starts = [block_start(passed_ref[i : i + 1, :]) for i in range(n)]
    cut(starts, depth_tiles, cols, anchors_ref, panel_ref, refs)


def split(x):
    high = x.astype(jnp.bfloat16)
    return high, (x - high.astype(jnp.float32)).astype(jnp.bfloat16)


def rows_kernel(rows_ref, slot_ref, turned_ref, scale_ref, bias_ref):
    rows, depth = rows_ref.shape
    tile = math.gcd(rows, 256)
    for t in range(rows // tile):
        span = slice(t * tile, (t + 1) * tile)
        turned = jnp.transpose(rows_ref[span, :])
        turned_ref[:, span] = turned
        wide = turned.astype(jnp.float32)
        mean = jnp.sum(wide * wide, axis=0, keepdims=True) / depth
        scale_ref[:, span] = jnp.broadcast_to(lax.rsqrt(mean + EPS), (8, tile))
    step, place = divide(slot_ref[...], BA)
    iota = lax.broadcasted_iota(jnp.int32, (BA, rows), 0).astype(jnp.bfloat16)
    for s in range(bias_ref.shape[0] // BA):
        key = jnp.where(step == s, place, -1).astype(jnp.bfloat16)
        bias = jnp.full(iota.shape, MISS, jnp.bfloat16)
        for k in range(slot_ref.shape[0]):
            bias = jnp.where(iota == key[k : k + 1, :], jnp.bfloat16(0), bias)
        bias_ref[s * BA : (s + 1) * BA, :] = bias


def group_body(steps, depth, cols, tile, messages, rows_ref, bias_ref, scale_ref, before, total_ref, high_ref, low_ref):
    depth_tiles = depth // LANES
    count = len(messages) * BA
    blocks, panels, scales = [], [], []
    for m in messages:
        block = jnp.concatenate([m[j * BA : (j + 1) * BA, :] for j in range(depth_tiles)], axis=1)
        wide = block.astype(jnp.float32)
        mean = jnp.sum(wide * wide, axis=1, keepdims=True) / depth
        scales.append(lax.rsqrt(mean + EPS) * (math.log2(math.e) / TEMPERATURE / depth))
        blocks.append(block)
        panels.append(m[depth_tiles * BA : depth_tiles * BA + cols, :])
    block = jnp.concatenate(blocks, axis=0)
    anchor_scale = jnp.concatenate(scales, axis=0)
    panel = jnp.concatenate(panels, axis=1)
    panel = jnp.concatenate([panel, jnp.ones((cols, count), jnp.bfloat16)], axis=0)
    for t in range(rows_ref.shape[1] // tile):
        span = slice(t * tile, (t + 1) * tile)
        dots = jnp.dot(block, rows_ref[:, span], preferred_element_type=jnp.float32)
        bias = jnp.concatenate([bias_ref[s * BA : (s + 1) * BA, span] for s in steps], axis=0)
        high, low = split(jnp.exp2(dots * anchor_scale * scale_ref[0:1, span] + bias.astype(jnp.float32)))
        high_ref[:, span] = high
        low_ref[:, span] = low
    for t in range(rows_ref.shape[1] // tile):
        span = slice(t * tile, (t + 1) * tile)
        part = jnp.dot(panel, high_ref[:, span], preferred_element_type=jnp.float32)
        part += jnp.dot(panel, low_ref[:, span], preferred_element_type=jnp.float32)
        total_ref[:, span] = part if before is None else before[:, span] + part


def group_kernel(steps, sizes, *refs):
    messages, refs = refs[: len(steps)], refs[len(steps) :]
    rows_ref, bias_ref, scale_ref = refs[:3]
    before = refs[3] if len(refs) == 7 else None
    group_body(steps, *sizes, messages, rows_ref, bias_ref, scale_ref, before, *refs[-3:])


def last_kernel(plan, copies, groups, sizes, *refs):
    steps = groups[-1]
    messages, refs = refs[: len(steps)], refs[len(steps) :]
    rows_ref, bias_ref, scale_ref, before, wanted_ref = refs[:5]
    parts = [*refs[5:-5], *refs[-3:-1]]
    out_ref, total, high_ref, low_ref, terms = refs[-5:]
    cols = sizes[1]
    group_body(steps, *sizes, messages, rows_ref, bias_ref, scale_ref, before, total, high_ref, low_ref)
    me = plan.me()
    inverse = 1.0 / total[cols : cols + 1, :]
    high, low = split(total[0:cols, :] * inverse * inverse)
    both = jnp.concatenate([high, low], axis=0)
    dims = (((1,), (1,)), ((), ()))
    for g, weights_high, weights_low in zip(groups, parts[0::2], parts[1::2], strict=True):
        main = lax.dot_general(both, weights_high[...], dims, preferred_element_type=jnp.float32)
        rest = lax.dot_general(high, weights_low[...], dims, preferred_element_type=jnp.float32)
        for b, step in enumerate(g):
            span, to = slice(b * BA, (b + 1) * BA), slice(step * BA, (step + 1) * BA)
            terms[:, to] = main[:cols, span] + main[cols:, span] + rest[:, span]
    size = cols // 2 + 1
    for owner in range(plan.owners):
        block = terms[:, pl.ds(pl.multiple_of((me ^ owner) * BA, BA), BA)]
        top = jnp.maximum(jnp.max(jnp.abs(block), axis=0, keepdims=True), 1e-30)
        code = jnp.ceil(jnp.log2(top) * STEPS_PER_OCTAVE)
        value = jnp.round(block * (jnp.exp2(code * (-1.0 / STEPS_PER_OCTAVE)) * FULL)).astype(jnp.int32)
        pairs = jnp.left_shift(value[: cols // 2, :], 16) | (value[cols // 2 :, :] & 0xFFFF)
        header = jnp.left_shift(code.astype(jnp.int32), 16) | wanted_ref[owner : owner + 1, :]
        message = jnp.concatenate([pairs, header], axis=0)
        for c in range(copies):
            at = (owner * copies + c) * size
            out_ref[at : at + size, :] = message


def sum_kernel(cols, messages_ref, out_ref):
    out_ref[...] = jnp.zeros_like(out_ref)
    half = cols // 2
    size = half + 1
    count = messages_ref.shape[0] // size
    batch = math.gcd(count, 32)

    def add(i, carry):
        part = messages_ref.at[pl.ds(pl.multiple_of(i * batch * size, 8), batch * size), :]
        headers = [part[d * size + half : (d + 1) * size, :] for d in range(batch)]
        places = [pl.multiple_of((h[0, 0] & 0xFFFF) * BA, BA) for h in headers]
        for d in range(batch):
            code = jnp.right_shift(headers[d], 16).astype(jnp.float32)
            scale = jnp.exp2(code * (1.0 / STEPS_PER_OCTAVE)) * (1.0 / FULL)
            pairs = part[d * size : d * size + half, :]
            first = jnp.right_shift(pairs, 16).astype(jnp.float32)
            second = jnp.right_shift(jnp.left_shift(pairs, 16), 16).astype(jnp.float32)
            out_ref[:half, pl.ds(places[d], BA)] += first * scale
            out_ref[half:, pl.ds(places[d], BA)] += second * scale
        return carry

    lax.fori_loop(0, count // batch, add, 0, unroll=count == batch)


def per_device(embeddings, anchors, subspace, nearest):
    plan = Plan(lax.axis_size("arow"), lax.axis_size("acol"))
    copies = lax.axis_size("samp")
    owners = plan.owners
    shard, depth = anchors.shape
    cols = subspace.shape[1]
    rows, cand = nearest.shape
    depth_tiles = depth // LANES
    f32, bf16, i32 = jnp.float32, jnp.bfloat16, jnp.int32
    struct = jax.ShapeDtypeStruct

    panel = subspace.T
    slot, wanted = pl.pallas_call(
        functools.partial(prepare_kernel, plan, shard),
        out_shape=(struct((cand, rows), i32), struct((owners, LANES), i32)),
        in_specs=[VMEM],
        out_specs=(VMEM, VMEM),
        compiler_params=params(4),
        name="prepare",
    )(nearest.T)
    here = ("arow", "acol")
    tile = math.gcd(rows, 256)

    message = struct((depth_tiles * BA + cols, LANES), bf16)
    even, odd = plan.even(), plan.odd()
    half = len(even)
    staged = pl.pallas_call(
        stage_kernel,
        out_shape=(struct(anchors.shape, bf16), struct(panel.shape, bf16)),
        in_specs=[VMEM, HBM, HBM],
        out_specs=(VMEM, VMEM),
        scratch_shapes=[pltpu.SemaphoreType.DMA((2,))],
        cost_estimate=QUICK,
        compiler_params=params(LIMIT_STAGE),
        name="stage",
    )(wanted, anchors, panel)
    passed = struct((-(-half // 8) * 8, LANES), i32)
    asked = [wanted, *(lax.ppermute(wanted, here, plan.pairs(s)) for s in even[1:])]
    *sent_even, passed = pl.pallas_call(
        functools.partial(even_kernel, plan, depth_tiles, cols),
        out_shape=(*(message,) * half, passed),
        in_specs=[VMEM] * (half + 2),
        out_specs=(VMEM,) * (half + 1),
        cost_estimate=QUICK,
        compiler_params=params(4),
        name="cut_even",
    )(*asked, *staged)
    passed = lax.ppermute(passed, here, plan.pairs(1))
    sent_odd = pl.pallas_call(
        functools.partial(odd_kernel, plan, depth_tiles, cols),
        out_shape=(message,) * half,
        in_specs=[VMEM] * 3,
        out_specs=(VMEM,) * half,
        cost_estimate=QUICK,
        compiler_params=params(4),
        name="cut_odd",
    )(passed, *staged)
    slot, *sent_odd = lax.optimization_barrier((slot, *sent_odd))
    sent = {**dict(zip(even, sent_even)), **dict(zip(odd, sent_odd))}
    turned, scale, bias = pl.pallas_call(
        rows_kernel,
        out_shape=(struct((depth, rows), bf16), struct((8, rows), f32), struct((owners * BA, rows), bf16)),
        in_specs=[VMEM, VMEM],
        out_specs=(VMEM,) * 3,
        cost_estimate=QUICK,
        compiler_params=params(16),
        name="rows",
        )(embeddings, slot)

    sizes = (depth, cols, tile)

    def weigh(g, state):
        n = len(g) * BA
        return pl.pallas_call(
            functools.partial(group_kernel, g, sizes),
            out_shape=(struct((2 * cols, rows), f32), struct((n, rows), bf16), struct((n, rows), bf16)),
            in_specs=[VMEM] * (len(g) + 3 + len(state)),
            out_specs=(VMEM,) * 3,
            cost_estimate=QUICK,
            compiler_params=params(10),
            name="weights",
        )(*[held[s] for s in g], turned, bias, scale, *state)

    groups = plan.groups()
    held, total, parts = {0: sent[0]}, None, []
    for s, after in plan.order():
        block = sent[s]
        if after:
            block, *_ = lax.optimization_barrier((block, held[after]))
        held[s] = lax.ppermute(block, here, plan.pairs(s))
    for g in groups[:-1]:
        total, high, low = weigh(g, [] if total is None else [total])
        parts += [high, low]
    g = groups[-1]
    n = len(g) * BA
    small = owners * BA * rows * 4 <= 8 * MIB
    terms = pl.pallas_call(
        functools.partial(last_kernel, plan, copies, groups, sizes),
        out_shape=struct((copies * owners * (cols // 2 + 1), BA), i32),
        in_specs=[VMEM] * (len(g) + 5 + len(parts)),
        out_specs=VMEM,
        cost_estimate=QUICK,
        scratch_shapes=[pltpu.VMEM((2 * cols, rows), f32), pltpu.VMEM((n, rows), bf16), pltpu.VMEM((n, rows), bf16), pltpu.VMEM((cols, owners * BA), f32)],
        compiler_params=params(14 if small else 60),
        name="terms",
    )(*[held[s] for s in g], turned, bias, scale, total, wanted, *parts)
    returned = lax.all_to_all(terms[:, None, :], ("arow", "acol", "samp"), 0, 0, tiled=True)[:, 0, :]
    result = pl.pallas_call(
        functools.partial(sum_kernel, cols),
        out_shape=struct((cols, shard), f32),
        in_specs=[VMEM],
        out_specs=VMEM,
        compiler_params=params(16),
        name="sum_terms",
    )(returned)
    return result.T


def solution(mesh):
    in_specs = (
        P(("samp", "arow", "acol"), None),
        P(("arow", "acol"), None),
        P(("arow", "acol"), None),
        P(("samp", "arow", "acol"), None),
    )
    return jax.shard_map(
        per_device, mesh=mesh, in_specs=in_specs, out_specs=P(("arow", "acol"), None), check_vma=False
    )
```

```python
import functools
import math

import jax
import jax.numpy as jnp
from jax import lax
from jax.experimental import pallas as pl
from jax.experimental.pallas import tpu as pltpu
from jax.sharding import PartitionSpec as P

BA = 128
EPS = 1e-6
TEMPERATURE = 0.05
LANES = 128
MISS = -1e30
ORDER = [(2, 0), (4, 0), (6, 0), (3, 0), (5, 0), (7, 2), (1, 4)]
GROUPS = [[0, 2], [1, 4], [5], [3, 6], [7]]
IN_FLIGHT = 5
FULL = 32704.0
STEPS_PER_OCTAVE = 256.0
MIB = 1024 * 1024

VMEM = pl.BlockSpec(memory_space=pltpu.VMEM)
SMEM = pl.BlockSpec(memory_space=pltpu.SMEM)
ANY = pl.BlockSpec(memory_space=pl.ANY)
HBM = pl.BlockSpec(memory_space=pltpu.HBM)
LONG = pl.CostEstimate(flops=2**33, bytes_accessed=2**22, transcendentals=0)
QUICK = pl.CostEstimate(flops=1, bytes_accessed=1, transcendentals=0)


def divide(x, by):
    if by & (by - 1) == 0:
        return lax.shift_right_logical(x, by.bit_length() - 1), x & (by - 1)
    quotient = lax.div(x, jnp.int32(by))
    return quotient, x - quotient * by


def params(limit_mib, **more):
    return pltpu.CompilerParams(vmem_limit_bytes=int(limit_mib * MIB), **more)


class Plan:
    def __init__(self, rows, cols):
        self.cols = cols
        self.owners = rows * cols
        assert self.owners & (self.owners - 1) == 0 and cols % 2 == 0

    def me(self):
        return lax.axis_index("arow") * self.cols + lax.axis_index("acol")

    def even(self):
        return list(range(0, self.owners, 2))

    def odd(self):
        return list(range(1, self.owners, 2))

    def order(self):
        if self.owners == 8:
            return ORDER
        steps = [*self.even()[1:], *self.odd()]
        return [(s, steps[i - IN_FLIGHT] if i >= IN_FLIGHT else 0) for i, s in enumerate(steps)]

    def groups(self):
        if self.owners == 8:
            return GROUPS
        order = [s for s, _ in self.order()]
        return [[0], *(order[i : min(i + 2, len(order) - 1)] for i in range(0, len(order) - 1, 2)), order[-1:]]

    def pairs(self, step):
        return [(i, i ^ step) for i in range(self.owners)]


def prepare_kernel(plan, shard, near_ref, slot_ref, wanted_ref):
    me = plan.me()
    owner, within = divide(near_ref[...], shard)
    block, place = divide(within, BA)
    slot_ref[...] = (me ^ owner) * BA + place
    for o in range(plan.owners):
        picked = jnp.where(owner == o, block, 0)
        wanted_ref[o : o + 1, :] = jnp.full((1, LANES), jnp.max(picked), jnp.int32)


def cut(starts, depth_tiles, cols, anchors_ref, panel_ref, out):
    for i, start in enumerate(starts):
        for j in range(depth_tiles):
            out[i][j * BA : (j + 1) * BA, :] = anchors_ref[pl.ds(start, BA), j * LANES : (j + 1) * LANES]
        out[i][depth_tiles * BA :, :] = panel_ref[:, pl.ds(start, BA)]


def block_start(line):
    return pl.multiple_of(line[0, 0] * BA, BA)


def even_kernel(plan, depth_tiles, cols, *refs):
    n = len(plan.even())
    asked, (anchors_ref, panel_ref), out = refs[:n], refs[n : n + 2], refs[n + 2 : 2 * n + 2]
    passed_ref = refs[2 * n + 2]
    me = plan.me()
    starts = [block_start(a[pl.ds(me, 1), :]) for a in asked]
    passed_ref[...] = jnp.zeros_like(passed_ref)
    for s, a in zip(plan.even(), asked):
        passed_ref[s // 2 : s // 2 + 1, :] = a[pl.ds(me ^ 1, 1), :]
    cut(starts, depth_tiles, cols, anchors_ref, panel_ref, out)


def odd_kernel(plan, depth_tiles, cols, passed_ref, anchors_ref, panel_ref, *refs):
    n = len(plan.odd())
    starts = [block_start(passed_ref[i : i + 1, :]) for i in range(n)]
    cut(starts, depth_tiles, cols, anchors_ref, panel_ref, refs)


def split(x):
    high = x.astype(jnp.bfloat16)
    return high, (x - high.astype(jnp.float32)).astype(jnp.bfloat16)


def rows_kernel(rows_ref, slot_ref, turned_ref, scale_ref, bias_ref):
    rows, depth = rows_ref.shape
    tile = math.gcd(rows, 256)
    for t in range(rows // tile):
        span = slice(t * tile, (t + 1) * tile)
        turned = jnp.transpose(rows_ref[span, :])
        turned_ref[:, span] = turned
        wide = turned.astype(jnp.float32)
        mean = jnp.sum(wide * wide, axis=0, keepdims=True) / depth
        scale_ref[:, span] = jnp.broadcast_to(lax.rsqrt(mean + EPS), (8, tile))
    step, place = divide(slot_ref[...], BA)
    iota = lax.broadcasted_iota(jnp.int32, (BA, rows), 0).astype(jnp.bfloat16)
    for s in range(bias_ref.shape[0] // BA):
        key = jnp.where(step == s, place, -1).astype(jnp.bfloat16)
        bias = jnp.full(iota.shape, MISS, jnp.bfloat16)
        for k in range(slot_ref.shape[0]):
            bias = jnp.where(iota == key[k : k + 1, :], jnp.bfloat16(0), bias)
        bias_ref[s * BA : (s + 1) * BA, :] = bias


def group_body(steps, depth, cols, tile, messages, rows_ref, bias_ref, scale_ref, before, total_ref, high_ref, low_ref):
    depth_tiles = depth // LANES
    count = len(messages) * BA
    blocks, panels, scales = [], [], []
    for m in messages:
        block = jnp.concatenate([m[j * BA : (j + 1) * BA, :] for j in range(depth_tiles)], axis=1)
        wide = block.astype(jnp.float32)
        mean = jnp.sum(wide * wide, axis=1, keepdims=True) / depth
        scales.append(lax.rsqrt(mean + EPS) * (math.log2(math.e) / TEMPERATURE / depth))
        blocks.append(block)
        panels.append(m[depth_tiles * BA : depth_tiles * BA + cols, :])
    block = jnp.concatenate(blocks, axis=0)
    anchor_scale = jnp.concatenate(scales, axis=0)
    panel = jnp.concatenate(panels, axis=1)
    panel = jnp.concatenate([panel, jnp.ones((cols, count), jnp.bfloat16)], axis=0)
    for t in range(rows_ref.shape[1] // tile):
        span = slice(t * tile, (t + 1) * tile)
        dots = jnp.dot(block, rows_ref[:, span], preferred_element_type=jnp.float32)
        bias = jnp.concatenate([bias_ref[s * BA : (s + 1) * BA, span] for s in steps], axis=0)
        high, low = split(jnp.exp2(dots * anchor_scale * scale_ref[0:1, span] + bias.astype(jnp.float32)))
        high_ref[:, span] = high
        low_ref[:, span] = low
    for t in range(rows_ref.shape[1] // tile):
        span = slice(t * tile, (t + 1) * tile)
        part = jnp.dot(panel, high_ref[:, span], preferred_element_type=jnp.float32)
        part += jnp.dot(panel, low_ref[:, span], preferred_element_type=jnp.float32)
        total_ref[:, span] = part if before is None else before[:, span] + part


def group_kernel(steps, sizes, *refs):
    messages, refs = refs[: len(steps)], refs[len(steps) :]
    rows_ref, bias_ref, scale_ref = refs[:3]
    before = refs[3] if len(refs) == 7 else None
    group_body(steps, *sizes, messages, rows_ref, bias_ref, scale_ref, before, *refs[-3:])


def last_kernel(plan, copies, groups, sizes, *refs):
    steps = groups[-1]
    messages, refs = refs[: len(steps)], refs[len(steps) :]
    rows_ref, bias_ref, scale_ref, before, wanted_ref = refs[:5]
    parts = [*refs[5:-5], *refs[-3:-1]]
    out_ref, total, high_ref, low_ref, terms = refs[-5:]
    cols = sizes[1]
    group_body(steps, *sizes, messages, rows_ref, bias_ref, scale_ref, before, total, high_ref, low_ref)
    me = plan.me()
    inverse = 1.0 / total[cols : cols + 1, :]
    high, low = split(total[0:cols, :] * inverse * inverse)
    both = jnp.concatenate([high, low], axis=0)
    dims = (((1,), (1,)), ((), ()))
    for g, weights_high, weights_low in zip(groups, parts[0::2], parts[1::2], strict=True):
        main = lax.dot_general(both, weights_high[...], dims, preferred_element_type=jnp.float32)
        rest = lax.dot_general(high, weights_low[...], dims, preferred_element_type=jnp.float32)
        for b, step in enumerate(g):
            span, to = slice(b * BA, (b + 1) * BA), slice(step * BA, (step + 1) * BA)
            terms[:, to] = main[:cols, span] + main[cols:, span] + rest[:, span]
    size = cols // 2 + 1
    for owner in range(plan.owners):
        block = terms[:, pl.ds(pl.multiple_of((me ^ owner) * BA, BA), BA)]
        top = jnp.maximum(jnp.max(jnp.abs(block), axis=0, keepdims=True), 1e-30)
        code = jnp.ceil(jnp.log2(top) * STEPS_PER_OCTAVE)
        value = jnp.round(block * (jnp.exp2(code * (-1.0 / STEPS_PER_OCTAVE)) * FULL)).astype(jnp.int32)
        pairs = jnp.left_shift(value[: cols // 2, :], 16) | (value[cols // 2 :, :] & 0xFFFF)
        header = jnp.left_shift(code.astype(jnp.int32), 16) | wanted_ref[owner : owner + 1, :]
        message = jnp.concatenate([pairs, header], axis=0)
        for c in range(copies):
            at = (owner * copies + c) * size
            out_ref[at : at + size, :] = message


def sum_kernel(cols, messages_ref, out_ref):
    out_ref[...] = jnp.zeros_like(out_ref)
    half = cols // 2
    size = half + 1
    count = messages_ref.shape[0] // size
    batch = math.gcd(count, 32)

    def add(i, carry):
        part = messages_ref.at[pl.ds(pl.multiple_of(i * batch * size, 8), batch * size), :]
        headers = [part[d * size + half : (d + 1) * size, :] for d in range(batch)]
        places = [pl.multiple_of((h[0, 0] & 0xFFFF) * BA, BA) for h in headers]
        for d in range(batch):
            code = jnp.right_shift(headers[d], 16).astype(jnp.float32)
            scale = jnp.exp2(code * (1.0 / STEPS_PER_OCTAVE)) * (1.0 / FULL)
            pairs = part[d * size : d * size + half, :]
            first = jnp.right_shift(pairs, 16).astype(jnp.float32)
            second = jnp.right_shift(jnp.left_shift(pairs, 16), 16).astype(jnp.float32)
            out_ref[:half, pl.ds(places[d], BA)] += first * scale
            out_ref[half:, pl.ds(places[d], BA)] += second * scale
        return carry

    lax.fori_loop(0, count // batch, add, 0, unroll=count == batch)


def per_device(embeddings, anchors, subspace, nearest):
    plan = Plan(lax.axis_size("arow"), lax.axis_size("acol"))
    copies = lax.axis_size("samp")
    owners = plan.owners
    shard, depth = anchors.shape
    cols = subspace.shape[1]
    rows, cand = nearest.shape
    depth_tiles = depth // LANES
    f32, bf16, i32 = jnp.float32, jnp.bfloat16, jnp.int32
    struct = jax.ShapeDtypeStruct

    panel = subspace.T
    slot, wanted = pl.pallas_call(
        functools.partial(prepare_kernel, plan, shard),
        out_shape=(struct((cand, rows), i32), struct((owners, LANES), i32)),
        in_specs=[VMEM],
        out_specs=(VMEM, VMEM),
        cost_estimate=LONG,
        compiler_params=params(4),
        name="prepare",
    )(nearest.T)
    here = ("arow", "acol")
    tile = math.gcd(rows, 256)

    message = struct((depth_tiles * BA + cols, LANES), bf16)
    even, odd = plan.even(), plan.odd()
    half = len(even)
    passed = struct((-(-half // 8) * 8, LANES), i32)
    asked = [wanted, *(lax.ppermute(wanted, here, plan.pairs(s)) for s in even[1:])]
    *sent_even, passed = pl.pallas_call(
        functools.partial(even_kernel, plan, depth_tiles, cols),
        out_shape=(*(message,) * half, passed),
        in_specs=[VMEM] * (half + 2),
        out_specs=(VMEM,) * (half + 1),
        cost_estimate=QUICK,
        compiler_params=params(4),
        name="cut_even",
    )(*asked, anchors, panel)
    passed = lax.ppermute(passed, here, plan.pairs(1))
    sent_odd = pl.pallas_call(
        functools.partial(odd_kernel, plan, depth_tiles, cols),
        out_shape=(message,) * half,
        in_specs=[VMEM] * 3,
        out_specs=(VMEM,) * half,
        cost_estimate=QUICK,
        compiler_params=params(4),
        name="cut_odd",
    )(passed, anchors, panel)
    slot, *sent_odd = lax.optimization_barrier((slot, *sent_odd))
    sent = {**dict(zip(even, sent_even)), **dict(zip(odd, sent_odd))}
    turned, scale, bias = pl.pallas_call(
        rows_kernel,
        out_shape=(struct((depth, rows), bf16), struct((8, rows), f32), struct((owners * BA, rows), bf16)),
        in_specs=[VMEM, VMEM],
        out_specs=(VMEM,) * 3,
        cost_estimate=QUICK,
        compiler_params=params(16),
        name="rows",
        )(embeddings, slot)

    sizes = (depth, cols, tile)

    def weigh(g, state):
        n = len(g) * BA
        return pl.pallas_call(
            functools.partial(group_kernel, g, sizes),
            out_shape=(struct((2 * cols, rows), f32), struct((n, rows), bf16), struct((n, rows), bf16)),
            in_specs=[VMEM] * (len(g) + 3 + len(state)),
            out_specs=(VMEM,) * 3,
            cost_estimate=QUICK,
            compiler_params=params(10),
            name="weights",
        )(*[held[s] for s in g], turned, bias, scale, *state)

    groups = plan.groups()
    held, total, parts = {0: sent[0]}, None, []
    for s, after in plan.order():
        block = sent[s]
        if after:
            block, *_ = lax.optimization_barrier((block, held[after]))
        held[s] = lax.ppermute(block, here, plan.pairs(s))
    for g in groups[:-1]:
        total, high, low = weigh(g, [] if total is None else [total])
        parts += [high, low]
    g = groups[-1]
    n = len(g) * BA
    small = owners * BA * rows * 4 <= 8 * MIB
    terms = pl.pallas_call(
        functools.partial(last_kernel, plan, copies, groups, sizes),
        out_shape=struct((copies * owners * (cols // 2 + 1), BA), i32),
        in_specs=[VMEM] * (len(g) + 5 + len(parts)),
        out_specs=VMEM,
        cost_estimate=QUICK,
        scratch_shapes=[pltpu.VMEM((2 * cols, rows), f32), pltpu.VMEM((n, rows), bf16), pltpu.VMEM((n, rows), bf16), pltpu.VMEM((cols, owners * BA), f32)],
        compiler_params=params(14 if small else 60),
        name="terms",
    )(*[held[s] for s in g], turned, bias, scale, total, wanted, *parts)
    returned = lax.all_to_all(terms[:, None, :], ("arow", "acol", "samp"), 0, 0, tiled=True)[:, 0, :]
    result = pl.pallas_call(
        functools.partial(sum_kernel, cols),
        out_shape=struct((cols, shard), f32),
        in_specs=[VMEM],
        out_specs=VMEM,
        compiler_params=params(16),
        name="sum_terms",
    )(returned)
    return result.T


def solution(mesh):
    in_specs = (
        P(("samp", "arow", "acol"), None),
        P(("arow", "acol"), None),
        P(("arow", "acol"), None),
        P(("samp", "arow", "acol"), None),
    )
    return jax.shard_map(
        per_device, mesh=mesh, in_specs=in_specs, out_specs=P(("arow", "acol"), None), check_vma=False
    )
```

```python
import functools
import math

import jax
import jax.numpy as jnp
from jax import lax
from jax.experimental import pallas as pl
from jax.experimental.pallas import tpu as pltpu
from jax.sharding import PartitionSpec as P

BA = 128
EPS = 1e-6
TEMPERATURE = 0.05
LANES = 128
MISS = -1e30
ORDER = [(2, 0), (4, 0), (6, 0), (3, 0), (5, 0), (7, 4), (1, 4)]
GROUPS = [[0, 2], [4], [1, 3], [5, 6], [7]]
IN_FLIGHT = 5
FULL = 32704.0
STEPS_PER_OCTAVE = 256.0
MIB = 1024 * 1024

VMEM = pl.BlockSpec(memory_space=pltpu.VMEM)
SMEM = pl.BlockSpec(memory_space=pltpu.SMEM)
ANY = pl.BlockSpec(memory_space=pl.ANY)
HBM = pl.BlockSpec(memory_space=pltpu.HBM)
LONG = pl.CostEstimate(flops=2**33, bytes_accessed=2**22, transcendentals=0)
QUICK = pl.CostEstimate(flops=1, bytes_accessed=1, transcendentals=0)


def divide(x, by):
    if by & (by - 1) == 0:
        return lax.shift_right_logical(x, by.bit_length() - 1), x & (by - 1)
    quotient = lax.div(x, jnp.int32(by))
    return quotient, x - quotient * by


def params(limit_mib, **more):
    return pltpu.CompilerParams(vmem_limit_bytes=int(limit_mib * MIB), **more)


class Plan:
    def __init__(self, rows, cols):
        self.cols = cols
        self.owners = rows * cols
        assert self.owners & (self.owners - 1) == 0 and cols % 2 == 0

    def me(self):
        return lax.axis_index("arow") * self.cols + lax.axis_index("acol")

    def even(self):
        return list(range(0, self.owners, 2))

    def odd(self):
        return list(range(1, self.owners, 2))

    def order(self):
        if self.owners == 8:
            return ORDER
        steps = [*self.even()[1:], *self.odd()]
        return [(s, steps[i - IN_FLIGHT] if i >= IN_FLIGHT else 0) for i, s in enumerate(steps)]

    def groups(self):
        if self.owners == 8:
            return GROUPS
        order = [s for s, _ in self.order()]
        return [[0], *(order[i : min(i + 2, len(order) - 1)] for i in range(0, len(order) - 1, 2)), order[-1:]]

    def pairs(self, step):
        return [(i, i ^ step) for i in range(self.owners)]


def prepare_kernel(plan, shard, near_ref, slot_ref, wanted_ref):
    me = plan.me()
    owner, within = divide(near_ref[...], shard)
    block, place = divide(within, BA)
    slot_ref[...] = (me ^ owner) * BA + place
    for o in range(plan.owners):
        picked = jnp.where(owner == o, block, 0)
        wanted_ref[o : o + 1, :] = jnp.full((1, LANES), jnp.max(picked), jnp.int32)


def cut(starts, depth_tiles, cols, anchors_ref, panel_ref, out):
    for i, start in enumerate(starts):
        for j in range(depth_tiles):
            out[i][j * BA : (j + 1) * BA, :] = anchors_ref[pl.ds(start, BA), j * LANES : (j + 1) * LANES]
        out[i][depth_tiles * BA :, :] = panel_ref[:, pl.ds(start, BA)]


def block_start(line):
    return pl.multiple_of(line[0, 0] * BA, BA)


def even_kernel(plan, depth_tiles, cols, *refs):
    n = len(plan.even())
    asked, (anchors_ref, panel_ref), out = refs[:n], refs[n : n + 2], refs[n + 2 : 2 * n + 2]
    passed_ref = refs[2 * n + 2]
    me = plan.me()
    starts = [block_start(a[pl.ds(me, 1), :]) for a in asked]
    passed_ref[...] = jnp.zeros_like(passed_ref)
    for s, a in zip(plan.even(), asked):
        passed_ref[s // 2 : s // 2 + 1, :] = a[pl.ds(me ^ 1, 1), :]
    cut(starts, depth_tiles, cols, anchors_ref, panel_ref, out)


def odd_kernel(plan, depth_tiles, cols, passed_ref, anchors_ref, panel_ref, *refs):
    n = len(plan.odd())
    starts = [block_start(passed_ref[i : i + 1, :]) for i in range(n)]
    cut(starts, depth_tiles, cols, anchors_ref, panel_ref, refs)


def split(x):
    high = x.astype(jnp.bfloat16)
    return high, (x - high.astype(jnp.float32)).astype(jnp.bfloat16)


def rows_kernel(rows_ref, slot_ref, turned_ref, scale_ref, bias_ref):
    rows, depth = rows_ref.shape
    tile = math.gcd(rows, 256)
    for t in range(rows // tile):
        span = slice(t * tile, (t + 1) * tile)
        turned = jnp.transpose(rows_ref[span, :])
        turned_ref[:, span] = turned
        wide = turned.astype(jnp.float32)
        mean = jnp.sum(wide * wide, axis=0, keepdims=True) / depth
        scale_ref[:, span] = jnp.broadcast_to(lax.rsqrt(mean + EPS), (8, tile))
    step, place = divide(slot_ref[...], BA)
    iota = lax.broadcasted_iota(jnp.int32, (BA, rows), 0).astype(jnp.bfloat16)
    for s in range(bias_ref.shape[0] // BA):
        key = jnp.where(step == s, place, -1).astype(jnp.bfloat16)
        bias = jnp.full(iota.shape, MISS, jnp.bfloat16)
        for k in range(slot_ref.shape[0]):
            bias = jnp.where(iota == key[k : k + 1, :], jnp.bfloat16(0), bias)
        bias_ref[s * BA : (s + 1) * BA, :] = bias


def group_body(steps, depth, cols, tile, messages, rows_ref, bias_ref, scale_ref, before, total_ref, high_ref, low_ref):
    depth_tiles = depth // LANES
    count = len(messages) * BA
    blocks, panels, scales = [], [], []
    for m in messages:
        block = jnp.concatenate([m[j * BA : (j + 1) * BA, :] for j in range(depth_tiles)], axis=1)
        wide = block.astype(jnp.float32)
        mean = jnp.sum(wide * wide, axis=1, keepdims=True) / depth
        scales.append(lax.rsqrt(mean + EPS) * (math.log2(math.e) / TEMPERATURE / depth))
        blocks.append(block)
        panels.append(m[depth_tiles * BA : depth_tiles * BA + cols, :])
    block = jnp.concatenate(blocks, axis=0)
    anchor_scale = jnp.concatenate(scales, axis=0)
    panel = jnp.concatenate(panels, axis=1)
    panel = jnp.concatenate([panel, jnp.ones((cols, count), jnp.bfloat16)], axis=0)
    twice = jnp.concatenate([panel, panel], axis=1)
    for t in range(rows_ref.shape[1] // tile):
        span = slice(t * tile, (t + 1) * tile)
        dots = jnp.dot(block, rows_ref[:, span], preferred_element_type=jnp.float32)
        bias = jnp.concatenate([bias_ref[s * BA : (s + 1) * BA, span] for s in steps], axis=0)
        high, low = split(jnp.exp2(dots * anchor_scale * scale_ref[0:1, span] + bias.astype(jnp.float32)))
        high_ref[:, span] = high
        low_ref[:, span] = low
    for t in range(rows_ref.shape[1] // tile):
        span = slice(t * tile, (t + 1) * tile)
        if count < 2 * BA:
            weights = jnp.concatenate([high_ref[:, span], low_ref[:, span]], axis=0)
            part = jnp.dot(twice, weights, preferred_element_type=jnp.float32)
        else:
            part = jnp.dot(panel, high_ref[:, span], preferred_element_type=jnp.float32)
            part += jnp.dot(panel, low_ref[:, span], preferred_element_type=jnp.float32)
        total_ref[:, span] = part if before is None else before[:, span] + part


def group_kernel(steps, sizes, *refs):
    messages, refs = refs[: len(steps)], refs[len(steps) :]
    rows_ref, bias_ref, scale_ref = refs[:3]
    before = refs[3] if len(refs) == 7 else None
    group_body(steps, *sizes, messages, rows_ref, bias_ref, scale_ref, before, *refs[-3:])


def last_kernel(plan, copies, groups, sizes, *refs):
    steps = groups[-1]
    messages, refs = refs[: len(steps)], refs[len(steps) :]
    rows_ref, bias_ref, scale_ref, before, wanted_ref = refs[:5]
    parts = [*refs[5:-5], *refs[-3:-1]]
    out_ref, total, high_ref, low_ref, terms = refs[-5:]
    cols = sizes[1]
    group_body(steps, *sizes, messages, rows_ref, bias_ref, scale_ref, before, total, high_ref, low_ref)
    me = plan.me()
    inverse = 1.0 / total[cols : cols + 1, :]
    high, low = split(total[0:cols, :] * inverse * inverse)
    both = jnp.concatenate([high, low], axis=0)
    dims = (((1,), (1,)), ((), ()))
    for g, weights_high, weights_low in zip(groups, parts[0::2], parts[1::2], strict=True):
        main = lax.dot_general(both, weights_high[...], dims, preferred_element_type=jnp.float32)
        rest = lax.dot_general(high, weights_low[...], dims, preferred_element_type=jnp.float32)
        for b, step in enumerate(g):
            span, to = slice(b * BA, (b + 1) * BA), slice(step * BA, (step + 1) * BA)
            terms[:, to] = main[:cols, span] + main[cols:, span] + rest[:, span]
    size = cols // 2 + 1
    for owner in range(plan.owners):
        block = terms[:, pl.ds(pl.multiple_of((me ^ owner) * BA, BA), BA)]
        top = jnp.maximum(jnp.max(jnp.abs(block), axis=0, keepdims=True), 1e-30)
        code = jnp.ceil(jnp.log2(top) * STEPS_PER_OCTAVE)
        value = jnp.round(block * (jnp.exp2(code * (-1.0 / STEPS_PER_OCTAVE)) * FULL)).astype(jnp.int32)
        pairs = jnp.left_shift(value[: cols // 2, :], 16) | (value[cols // 2 :, :] & 0xFFFF)
        header = jnp.left_shift(code.astype(jnp.int32), 16) | wanted_ref[owner : owner + 1, :]
        message = jnp.concatenate([pairs, header], axis=0)
        for c in range(copies):
            at = (owner * copies + c) * size
            out_ref[at : at + size, :] = message


def sum_kernel(cols, messages_ref, out_ref):
    out_ref[...] = jnp.zeros_like(out_ref)
    half = cols // 2
    size = half + 1
    count = messages_ref.shape[0] // size
    batch = math.gcd(count, 32)

    def add(i, carry):
        part = messages_ref.at[pl.ds(pl.multiple_of(i * batch * size, 8), batch * size), :]
        headers = [part[d * size + half : (d + 1) * size, :] for d in range(batch)]
        places = [pl.multiple_of((h[0, 0] & 0xFFFF) * BA, BA) for h in headers]
        for d in range(batch):
            code = jnp.right_shift(headers[d], 16).astype(jnp.float32)
            scale = jnp.exp2(code * (1.0 / STEPS_PER_OCTAVE)) * (1.0 / FULL)
            pairs = part[d * size : d * size + half, :]
            first = jnp.right_shift(pairs, 16).astype(jnp.float32)
            second = jnp.right_shift(jnp.left_shift(pairs, 16), 16).astype(jnp.float32)
            out_ref[:half, pl.ds(places[d], BA)] += first * scale
            out_ref[half:, pl.ds(places[d], BA)] += second * scale
        return carry

    lax.fori_loop(0, count // batch, add, 0, unroll=count == batch)


def per_device(embeddings, anchors, subspace, nearest):
    plan = Plan(lax.axis_size("arow"), lax.axis_size("acol"))
    copies = lax.axis_size("samp")
    owners = plan.owners
    shard, depth = anchors.shape
    cols = subspace.shape[1]
    rows, cand = nearest.shape
    depth_tiles = depth // LANES
    f32, bf16, i32 = jnp.float32, jnp.bfloat16, jnp.int32
    struct = jax.ShapeDtypeStruct

    panel = subspace.T
    slot, wanted = pl.pallas_call(
        functools.partial(prepare_kernel, plan, shard),
        out_shape=(struct((cand, rows), i32), struct((owners, LANES), i32)),
        in_specs=[VMEM],
        out_specs=(VMEM, VMEM),
        cost_estimate=LONG,
        compiler_params=params(4),
        name="prepare",
    )(nearest.T)
    here = ("arow", "acol")
    tile = math.gcd(rows, 256)

    message = struct((depth_tiles * BA + cols, LANES), bf16)
    even, odd = plan.even(), plan.odd()
    half = len(even)
    passed = struct((-(-half // 8) * 8, LANES), i32)
    asked = [wanted, *(lax.ppermute(wanted, here, plan.pairs(s)) for s in even[1:])]
    *sent_even, passed = pl.pallas_call(
        functools.partial(even_kernel, plan, depth_tiles, cols),
        out_shape=(*(message,) * half, passed),
        in_specs=[VMEM] * (half + 2),
        out_specs=(VMEM,) * (half + 1),
        cost_estimate=QUICK,
        compiler_params=params(4),
        name="cut_even",
    )(*asked, anchors, panel)
    passed = lax.ppermute(passed, here, plan.pairs(1))
    sent_odd = pl.pallas_call(
        functools.partial(odd_kernel, plan, depth_tiles, cols),
        out_shape=(message,) * half,
        in_specs=[VMEM] * 3,
        out_specs=(VMEM,) * half,
        cost_estimate=QUICK,
        compiler_params=params(4),
        name="cut_odd",
    )(passed, anchors, panel)
    slot, *sent_odd = lax.optimization_barrier((slot, *sent_odd))
    sent = {**dict(zip(even, sent_even)), **dict(zip(odd, sent_odd))}
    turned, scale, bias = pl.pallas_call(
        rows_kernel,
        out_shape=(struct((depth, rows), bf16), struct((8, rows), f32), struct((owners * BA, rows), bf16)),
        in_specs=[VMEM, VMEM],
        out_specs=(VMEM,) * 3,
        cost_estimate=QUICK,
        compiler_params=params(16),
        name="rows",
        )(embeddings, slot)

    sizes = (depth, cols, tile)

    def weigh(g, state):
        n = len(g) * BA
        return pl.pallas_call(
            functools.partial(group_kernel, g, sizes),
            out_shape=(struct((2 * cols, rows), f32), struct((n, rows), bf16), struct((n, rows), bf16)),
            in_specs=[VMEM] * (len(g) + 3 + len(state)),
            out_specs=(VMEM,) * 3,
            cost_estimate=QUICK,
            compiler_params=params(10),
            name="weights",
        )(*[held[s] for s in g], turned, bias, scale, *state)

    groups = plan.groups()
    held, total, parts = {0: sent[0]}, None, []
    for s, after in plan.order():
        block = sent[s]
        if after:
            block, *_ = lax.optimization_barrier((block, held[after]))
        held[s] = lax.ppermute(block, here, plan.pairs(s))
    for g in groups[:-1]:
        total, high, low = weigh(g, [] if total is None else [total])
        parts += [high, low]
    g = groups[-1]
    n = len(g) * BA
    small = owners * BA * rows * 4 <= 8 * MIB
    terms = pl.pallas_call(
        functools.partial(last_kernel, plan, copies, groups, sizes),
        out_shape=struct((copies * owners * (cols // 2 + 1), BA), i32),
        in_specs=[VMEM] * (len(g) + 5 + len(parts)),
        out_specs=VMEM,
        cost_estimate=QUICK,
        scratch_shapes=[pltpu.VMEM((2 * cols, rows), f32), pltpu.VMEM((n, rows), bf16), pltpu.VMEM((n, rows), bf16), pltpu.VMEM((cols, owners * BA), f32)],
        compiler_params=params(14 if small else 60),
        name="terms",
    )(*[held[s] for s in g], turned, bias, scale, total, wanted, *parts)
    returned = lax.all_to_all(terms[:, None, :], ("arow", "acol", "samp"), 0, 0, tiled=True)[:, 0, :]
    result = pl.pallas_call(
        functools.partial(sum_kernel, cols),
        out_shape=struct((cols, shard), f32),
        in_specs=[VMEM],
        out_specs=VMEM,
        compiler_params=params(16),
        name="sum_terms",
    )(returned)
    return result.T


def solution(mesh):
    in_specs = (
        P(("samp", "arow", "acol"), None),
        P(("arow", "acol"), None),
        P(("arow", "acol"), None),
        P(("samp", "arow", "acol"), None),
    )
    return jax.shard_map(
        per_device, mesh=mesh, in_specs=in_specs, out_specs=P(("arow", "acol"), None), check_vma=False
    )
```

```python
import functools
import math

import jax
import jax.numpy as jnp
from jax import lax
from jax.experimental import pallas as pl
from jax.experimental.pallas import tpu as pltpu
from jax.sharding import PartitionSpec as P

BA = 128
EPS = 1e-6
TEMPERATURE = 0.05
LANES = 128
MISS = -1e30
ORDER = [(2, 0), (4, 0), (6, 0), (3, 0), (5, 0), (7, 4), (1, 4)]
GROUPS = [[0, 4], [2], [1, 3], [5, 6], [7]]
IN_FLIGHT = 5
FULL = 32704.0
STEPS_PER_OCTAVE = 256.0
MIB = 1024 * 1024

VMEM = pl.BlockSpec(memory_space=pltpu.VMEM)
SMEM = pl.BlockSpec(memory_space=pltpu.SMEM)
ANY = pl.BlockSpec(memory_space=pl.ANY)
HBM = pl.BlockSpec(memory_space=pltpu.HBM)
LONG = pl.CostEstimate(flops=2**33, bytes_accessed=2**22, transcendentals=0)
QUICK = pl.CostEstimate(flops=1, bytes_accessed=1, transcendentals=0)


def divide(x, by):
    if by & (by - 1) == 0:
        return lax.shift_right_logical(x, by.bit_length() - 1), x & (by - 1)
    quotient = lax.div(x, jnp.int32(by))
    return quotient, x - quotient * by


def params(limit_mib, **more):
    return pltpu.CompilerParams(vmem_limit_bytes=int(limit_mib * MIB), **more)


class Plan:
    def __init__(self, rows, cols):
        self.cols = cols
        self.owners = rows * cols
        assert self.owners & (self.owners - 1) == 0 and cols % 2 == 0

    def me(self):
        return lax.axis_index("arow") * self.cols + lax.axis_index("acol")

    def even(self):
        return list(range(0, self.owners, 2))

    def odd(self):
        return list(range(1, self.owners, 2))

    def order(self):
        if self.owners == 8:
            return ORDER
        steps = [*self.even()[1:], *self.odd()]
        return [(s, steps[i - IN_FLIGHT] if i >= IN_FLIGHT else 0) for i, s in enumerate(steps)]

    def groups(self):
        if self.owners == 8:
            return GROUPS
        order = [s for s, _ in self.order()]
        return [[0], *(order[i : min(i + 2, len(order) - 1)] for i in range(0, len(order) - 1, 2)), order[-1:]]

    def pairs(self, step):
        return [(i, i ^ step) for i in range(self.owners)]


def prepare_kernel(plan, shard, near_ref, slot_ref, wanted_ref):
    me = plan.me()
    owner, within = divide(near_ref[...], shard)
    block, place = divide(within, BA)
    slot_ref[...] = (me ^ owner) * BA + place
    for o in range(plan.owners):
        picked = jnp.where(owner == o, block, 0)
        wanted_ref[o : o + 1, :] = jnp.full((1, LANES), jnp.max(picked), jnp.int32)


def cut(starts, depth_tiles, cols, anchors_ref, panel_ref, out):
    for i, start in enumerate(starts):
        for j in range(depth_tiles):
            out[i][j * BA : (j + 1) * BA, :] = anchors_ref[pl.ds(start, BA), j * LANES : (j + 1) * LANES]
        out[i][depth_tiles * BA :, :] = panel_ref[:, pl.ds(start, BA)]


def block_start(line):
    return pl.multiple_of(line[0, 0] * BA, BA)


def even_kernel(plan, depth_tiles, cols, *refs):
    n = len(plan.even())
    asked, (anchors_ref, panel_ref), out = refs[:n], refs[n : n + 2], refs[n + 2 : 2 * n + 2]
    passed_ref = refs[2 * n + 2]
    me = plan.me()
    starts = [block_start(a[pl.ds(me, 1), :]) for a in asked]
    passed_ref[...] = jnp.zeros_like(passed_ref)
    for s, a in zip(plan.even(), asked):
        passed_ref[s // 2 : s // 2 + 1, :] = a[pl.ds(me ^ 1, 1), :]
    cut(starts, depth_tiles, cols, anchors_ref, panel_ref, out)


def odd_kernel(plan, depth_tiles, cols, passed_ref, anchors_ref, panel_ref, *refs):
    n = len(plan.odd())
    starts = [block_start(passed_ref[i : i + 1, :]) for i in range(n)]
    cut(starts, depth_tiles, cols, anchors_ref, panel_ref, refs)


def split(x):
    high = x.astype(jnp.bfloat16)
    return high, (x - high.astype(jnp.float32)).astype(jnp.bfloat16)


def rows_kernel(rows_ref, slot_ref, turned_ref, scale_ref, bias_ref):
    rows, depth = rows_ref.shape
    tile = math.gcd(rows, 256)
    for t in range(rows // tile):
        span = slice(t * tile, (t + 1) * tile)
        turned = jnp.transpose(rows_ref[span, :])
        turned_ref[:, span] = turned
        wide = turned.astype(jnp.float32)
        mean = jnp.sum(wide * wide, axis=0, keepdims=True) / depth
        scale_ref[:, span] = jnp.broadcast_to(lax.rsqrt(mean + EPS), (8, tile))
    step, place = divide(slot_ref[...], BA)
    iota = lax.broadcasted_iota(jnp.int32, (BA, rows), 0).astype(jnp.bfloat16)
    for s in range(bias_ref.shape[0] // BA):
        key = jnp.where(step == s, place, -1).astype(jnp.bfloat16)
        bias = jnp.full(iota.shape, MISS, jnp.bfloat16)
        for k in range(slot_ref.shape[0]):
            bias = jnp.where(iota == key[k : k + 1, :], jnp.bfloat16(0), bias)
        bias_ref[s * BA : (s + 1) * BA, :] = bias


def group_body(steps, depth, cols, tile, messages, rows_ref, bias_ref, scale_ref, before, total_ref, high_ref, low_ref):
    depth_tiles = depth // LANES
    count = len(messages) * BA
    blocks, panels, scales = [], [], []
    for m in messages:
        block = jnp.concatenate([m[j * BA : (j + 1) * BA, :] for j in range(depth_tiles)], axis=1)
        wide = block.astype(jnp.float32)
        mean = jnp.sum(wide * wide, axis=1, keepdims=True) / depth
        scales.append(lax.rsqrt(mean + EPS) * (math.log2(math.e) / TEMPERATURE / depth))
        blocks.append(block)
        panels.append(m[depth_tiles * BA : depth_tiles * BA + cols, :])
    block = jnp.concatenate(blocks, axis=0)
    anchor_scale = jnp.concatenate(scales, axis=0)
    panel = jnp.concatenate(panels, axis=1)
    panel = jnp.concatenate([panel, jnp.ones((cols, count), jnp.bfloat16)], axis=0)
    twice = jnp.concatenate([panel, panel], axis=1)
    for t in range(rows_ref.shape[1] // tile):
        span = slice(t * tile, (t + 1) * tile)
        dots = jnp.dot(block, rows_ref[:, span], preferred_element_type=jnp.float32)
        bias = jnp.concatenate([bias_ref[s * BA : (s + 1) * BA, span] for s in steps], axis=0)
        high, low = split(jnp.exp2(dots * anchor_scale * scale_ref[0:1, span] + bias.astype(jnp.float32)))
        high_ref[:, span] = high
        low_ref[:, span] = low
    for t in range(rows_ref.shape[1] // tile):
        span = slice(t * tile, (t + 1) * tile)
        if count < 2 * BA:
            weights = jnp.concatenate([high_ref[:, span], low_ref[:, span]], axis=0)
            part = jnp.dot(twice, weights, preferred_element_type=jnp.float32)
        else:
            part = jnp.dot(panel, high_ref[:, span], preferred_element_type=jnp.float32)
            part += jnp.dot(panel, low_ref[:, span], preferred_element_type=jnp.float32)
        total_ref[:, span] = part if before is None else before[:, span] + part


def group_kernel(steps, sizes, *refs):
    messages, refs = refs[: len(steps)], refs[len(steps) :]
    rows_ref, bias_ref, scale_ref = refs[:3]
    before = refs[3] if len(refs) == 7 else None
    group_body(steps, *sizes, messages, rows_ref, bias_ref, scale_ref, before, *refs[-3:])


def last_kernel(plan, copies, groups, sizes, *refs):
    steps = groups[-1]
    messages, refs = refs[: len(steps)], refs[len(steps) :]
    rows_ref, bias_ref, scale_ref, before, wanted_ref = refs[:5]
    parts = [*refs[5:-5], *refs[-3:-1]]
    out_ref, total, high_ref, low_ref, terms = refs[-5:]
    cols = sizes[1]
    group_body(steps, *sizes, messages, rows_ref, bias_ref, scale_ref, before, total, high_ref, low_ref)
    me = plan.me()
    inverse = 1.0 / total[cols : cols + 1, :]
    high, low = split(total[0:cols, :] * inverse * inverse)
    both = jnp.concatenate([high, low], axis=0)
    dims = (((1,), (1,)), ((), ()))
    for g, weights_high, weights_low in zip(groups, parts[0::2], parts[1::2], strict=True):
        main = lax.dot_general(both, weights_high[...], dims, preferred_element_type=jnp.float32)
        rest = lax.dot_general(high, weights_low[...], dims, preferred_element_type=jnp.float32)
        for b, step in enumerate(g):
            span, to = slice(b * BA, (b + 1) * BA), slice(step * BA, (step + 1) * BA)
            terms[:, to] = main[:cols, span] + main[cols:, span] + rest[:, span]
    size = cols // 2 + 1
    for owner in range(plan.owners):
        block = terms[:, pl.ds(pl.multiple_of((me ^ owner) * BA, BA), BA)]
        top = jnp.maximum(jnp.max(jnp.abs(block), axis=0, keepdims=True), 1e-30)
        code = jnp.ceil(jnp.log2(top) * STEPS_PER_OCTAVE)
        value = jnp.round(block * (jnp.exp2(code * (-1.0 / STEPS_PER_OCTAVE)) * FULL)).astype(jnp.int32)
        pairs = jnp.left_shift(value[: cols // 2, :], 16) | (value[cols // 2 :, :] & 0xFFFF)
        header = jnp.left_shift(code.astype(jnp.int32), 16) | wanted_ref[owner : owner + 1, :]
        message = jnp.concatenate([pairs, header], axis=0)
        for c in range(copies):
            at = (owner * copies + c) * size
            out_ref[at : at + size, :] = message


def sum_kernel(cols, messages_ref, out_ref):
    out_ref[...] = jnp.zeros_like(out_ref)
    half = cols // 2
    size = half + 1
    count = messages_ref.shape[0] // size
    batch = math.gcd(count, 32)

    def add(i, carry):
        part = messages_ref.at[pl.ds(pl.multiple_of(i * batch * size, 8), batch * size), :]
        headers = [part[d * size + half : (d + 1) * size, :] for d in range(batch)]
        places = [pl.multiple_of((h[0, 0] & 0xFFFF) * BA, BA) for h in headers]
        for d in range(batch):
            code = jnp.right_shift(headers[d], 16).astype(jnp.float32)
            scale = jnp.exp2(code * (1.0 / STEPS_PER_OCTAVE)) * (1.0 / FULL)
            pairs = part[d * size : d * size + half, :]
            first = jnp.right_shift(pairs, 16).astype(jnp.float32)
            second = jnp.right_shift(jnp.left_shift(pairs, 16), 16).astype(jnp.float32)
            out_ref[:half, pl.ds(places[d], BA)] += first * scale
            out_ref[half:, pl.ds(places[d], BA)] += second * scale
        return carry

    lax.fori_loop(0, count // batch, add, 0, unroll=count == batch)


def per_device(embeddings, anchors, subspace, nearest):
    plan = Plan(lax.axis_size("arow"), lax.axis_size("acol"))
    copies = lax.axis_size("samp")
    owners = plan.owners
    shard, depth = anchors.shape
    cols = subspace.shape[1]
    rows, cand = nearest.shape
    depth_tiles = depth // LANES
    f32, bf16, i32 = jnp.float32, jnp.bfloat16, jnp.int32
    struct = jax.ShapeDtypeStruct

    panel = subspace.T
    slot, wanted = pl.pallas_call(
        functools.partial(prepare_kernel, plan, shard),
        out_shape=(struct((cand, rows), i32), struct((owners, LANES), i32)),
        in_specs=[VMEM],
        out_specs=(VMEM, VMEM),
        cost_estimate=LONG,
        compiler_params=params(4),
        name="prepare",
    )(nearest.T)
    here = ("arow", "acol")
    tile = math.gcd(rows, 256)

    message = struct((depth_tiles * BA + cols, LANES), bf16)
    even, odd = plan.even(), plan.odd()
    half = len(even)
    passed = struct((-(-half // 8) * 8, LANES), i32)
    asked = [wanted, *(lax.ppermute(wanted, here, plan.pairs(s)) for s in even[1:])]
    *sent_even, passed = pl.pallas_call(
        functools.partial(even_kernel, plan, depth_tiles, cols),
        out_shape=(*(message,) * half, passed),
        in_specs=[VMEM] * (half + 2),
        out_specs=(VMEM,) * (half + 1),
        cost_estimate=QUICK,
        compiler_params=params(4),
        name="cut_even",
    )(*asked, anchors, panel)
    passed = lax.ppermute(passed, here, plan.pairs(1))
    sent_odd = pl.pallas_call(
        functools.partial(odd_kernel, plan, depth_tiles, cols),
        out_shape=(message,) * half,
        in_specs=[VMEM] * 3,
        out_specs=(VMEM,) * half,
        cost_estimate=QUICK,
        compiler_params=params(4),
        name="cut_odd",
    )(passed, anchors, panel)
    slot, *sent_odd = lax.optimization_barrier((slot, *sent_odd))
    sent = {**dict(zip(even, sent_even)), **dict(zip(odd, sent_odd))}
    turned, scale, bias = pl.pallas_call(
        rows_kernel,
        out_shape=(struct((depth, rows), bf16), struct((8, rows), f32), struct((owners * BA, rows), bf16)),
        in_specs=[VMEM, VMEM],
        out_specs=(VMEM,) * 3,
        cost_estimate=QUICK,
        compiler_params=params(16),
        name="rows",
        )(embeddings, slot)

    sizes = (depth, cols, tile)

    def weigh(g, state):
        n = len(g) * BA
        return pl.pallas_call(
            functools.partial(group_kernel, g, sizes),
            out_shape=(struct((2 * cols, rows), f32), struct((n, rows), bf16), struct((n, rows), bf16)),
            in_specs=[VMEM] * (len(g) + 3 + len(state)),
            out_specs=(VMEM,) * 3,
            cost_estimate=QUICK,
            compiler_params=params(10),
            name="weights",
        )(*[held[s] for s in g], turned, bias, scale, *state)

    groups = plan.groups()
    held, total, parts = {0: sent[0]}, None, []
    for s, after in plan.order():
        block = sent[s]
        if after:
            block, *_ = lax.optimization_barrier((block, held[after]))
        held[s] = lax.ppermute(block, here, plan.pairs(s))
    for g in groups[:-1]:
        total, high, low = weigh(g, [] if total is None else [total])
        parts += [high, low]
    g = groups[-1]
    n = len(g) * BA
    small = owners * BA * rows * 4 <= 8 * MIB
    terms = pl.pallas_call(
        functools.partial(last_kernel, plan, copies, groups, sizes),
        out_shape=struct((copies * owners * (cols // 2 + 1), BA), i32),
        in_specs=[VMEM] * (len(g) + 5 + len(parts)),
        out_specs=VMEM,
        cost_estimate=QUICK,
        scratch_shapes=[pltpu.VMEM((2 * cols, rows), f32), pltpu.VMEM((n, rows), bf16), pltpu.VMEM((n, rows), bf16), pltpu.VMEM((cols, owners * BA), f32)],
        compiler_params=params(14 if small else 60),
        name="terms",
    )(*[held[s] for s in g], turned, bias, scale, total, wanted, *parts)
    returned = lax.all_to_all(terms[:, None, :], ("arow", "acol", "samp"), 0, 0, tiled=True)[:, 0, :]
    result = pl.pallas_call(
        functools.partial(sum_kernel, cols),
        out_shape=struct((cols, shard), f32),
        in_specs=[VMEM],
        out_specs=VMEM,
        compiler_params=params(16),
        name="sum_terms",
    )(returned)
    return result.T


def solution(mesh):
    in_specs = (
        P(("samp", "arow", "acol"), None),
        P(("arow", "acol"), None),
        P(("arow", "acol"), None),
        P(("samp", "arow", "acol"), None),
    )
    return jax.shard_map(
        per_device, mesh=mesh, in_specs=in_specs, out_specs=P(("arow", "acol"), None), check_vma=False
    )
```
